128 devices in a mesh: src: 16 (over z, x), snk: 8 (over y, core).
Axes of the slice: x: 4, y: 4, z: 4, core: 2. Of those that a mesh axis runs over, the one named last changes fastest.
Arguments:
- perambulators: bfloat16 [16, 16, 2, 4, 128, 4, 128], P('src', 'snk'), may hold values from -6 to 6
- elementals: bfloat16 [16, 8, 2, 128, 128], P('src'), may hold values from -0.013671875 to 0.013671875
- gamma_codes: int32 [8], replicated, may hold values from 0 to 15
- momenta: int32 [8], replicated, may hold values from 0 to 3
- displacements: int32 [8], replicated, may hold values from 0 to 1
- sink_times: int32 [16], replicated, may hold values from 0 to 15, each once
Outputs:
- correlators: float32 [16, 16, 8, 8, 2], P('src', 'snk')
The draws below stay inside these ranges and needn't reach their ends.
Inputs may be any that keep to these rules, and one draw needn't show every extreme that they name: `sink_times`: each of the 16 times appears in exactly one slot.
All inputs are finite; a program needn't handle non-finite values.
Results may differ from the reference program's by a relative error of at most 0.0041.
Values may be sent and summed in bfloat16 or wider, within the bound.
No kernel may reach another device: no remote copies, remote signals or barrier semaphores. Data moves between devices by JAX's collectives and lax.ppermute only.
A program may use at most 192 MiB of HBM per device.

```python
import jax
import jax.numpy as jnp
import numpy as np
from jax import lax

NEV = 128
OPS = 8
NMOM = 4
NDISP = 2
NELEM = 8
NT = 16


def plant(entries, rng, least, top_value):
    shape = entries.shape
    index_at = [jax.random.randint(jax.random.fold_in(rng, axis), (), 0, shape[axis]) for axis in range(len(shape))]
    entries = entries.at[tuple(index_at)].set(least)
    longest = shape.index(max(shape))
    index_at[longest] = (index_at[longest] + 1) % shape[longest]
    return entries.at[tuple(index_at)].set(top_value)


def shard_levels(own_key, shape, pieces, smallest, top_value):
    def one(axis_at, parts):
        heights = jax.random.uniform(jax.random.fold_in(jax.random.fold_in(own_key, 6), axis_at), (parts,), jnp.float32, smallest / len(pieces), top_value / len(pieces))
        return jnp.repeat(jnp.exp(heights), shape[axis_at] // parts).reshape((-1,) + (1,) * (len(shape) - axis_at - 1))

    gain = one(*pieces[0])
    for cut in pieces[1:]:
        gain = gain * one(*cut)
    return gain


def normal_values(own_key, shape, width, reach, split=(), kind=jnp.bfloat16):
    result = width * jax.random.normal(own_key, shape, jnp.float32)
    if split:
        result = result * shard_levels(own_key, shape, split, -0.22, 0.18)
    return jnp.clip(result, -reach, reach).astype(kind)


def setup_inputs(seed: int = 0) -> dict:
    key_of = jax.random.split(jax.random.key(seed), 7)
    perambulators = normal_values(key_of[0], (NT, NT, 2, 4, NEV, 4, NEV), 1.0, 6.0, ((0, 16), (1, 8)))
    elementals = normal_values(key_of[1], (NT, NELEM, 2, NEV, NEV), (12 * NEV * NEV) ** -0.5, 0.013671875, ((0, 16),))
    gamma_codes = plant(jax.random.randint(key_of[2], (OPS,), 0, 16), jax.random.fold_in(key_of[2], 1), 0, 15).astype(jnp.int32)
    momenta = plant(jax.random.randint(key_of[3], (OPS,), 0, NMOM), jax.random.fold_in(key_of[3], 1), 0, NMOM - 1).astype(jnp.int32)
    displacements = plant(jax.random.randint(key_of[4], (OPS,), 0, NDISP), jax.random.fold_in(key_of[4], 1), 0, NDISP - 1).astype(jnp.int32)
    sink_times = jax.random.permutation(key_of[5], NT).astype(jnp.int32)
    return dict(perambulators=perambulators, elementals=elementals, gamma_codes=gamma_codes, momenta=momenta, displacements=displacements, sink_times=sink_times)


def off_diagonal(upper, lower):
    return np.array([[0, 0, upper[0, 0], upper[0, 1]], [0, 0, upper[1, 0], upper[1, 1]], [lower[0, 0], lower[0, 1], 0, 0], [lower[1, 0], lower[1, 1], 0, 0]], dtype=complex)


def gamma_tables():
    paulis = [np.array([[0, 1], [1, 0]], dtype=complex), np.array([[0, -1j], [1j, 0]], dtype=complex), np.array([[1, 0], [0, -1]], dtype=complex)]
    identity = np.eye(2, dtype=complex)
    gammas = [off_diagonal(-1j * matrix, 1j * matrix) for matrix in paulis]
    gammas.append(off_diagonal(identity, identity))
    gamma_table = []
    for gamma_code in range(16):
        product = np.eye(4, dtype=complex)
        for bit_index in range(4):
            if (gamma_code >> bit_index) & 1:
                product = product @ gammas[bit_index]
        gamma_table.append(product)
    gamma_table = np.stack(gamma_table)
    gamma_five = np.array([1.0, 1.0, -1.0, -1.0], dtype=np.float32)
    return gamma_table.real.astype(np.float32), gamma_table.imag.astype(np.float32), gamma_five


def operator_weights(gamma_codes, momenta, displacements, nelem, ndisp):
    table_real, table_imag, gamma_five = gamma_tables()
    gamma_pick = (gamma_codes[:, None] == jnp.arange(16, dtype=jnp.int32)[None, :]).astype(jnp.float32)
    gamma_real = jnp.einsum("ic,cab->iab", gamma_pick, jnp.asarray(table_real), precision=lax.Precision.HIGHEST)
    gamma_imag = jnp.einsum("ic,cab->iab", gamma_pick, jnp.asarray(table_imag), precision=lax.Precision.HIGHEST)
    elem_index = momenta * ndisp + displacements
    elem_pick = (elem_index[:, None] == jnp.arange(nelem, dtype=jnp.int32)[None, :]).astype(jnp.float32)
    w_real = gamma_real[:, :, None, :] * elem_pick[:, None, :, None]
    w_imag = gamma_imag[:, :, None, :] * elem_pick[:, None, :, None]
    return w_real, w_imag, jnp.asarray(gamma_five)


def high_dot(left, right):
    return jnp.dot(left, right, precision=lax.Precision.HIGHEST, preferred_element_type=jnp.float32)


def sink_side(peramb, elemental, w_real, w_imag):
    nev = elemental.shape[-1]
    tau_real = peramb[0].reshape(4, nev, 4 * nev)
    tau_imag = peramb[1].reshape(4, nev, 4 * nev)
    el_real = elemental[:, 0]
    el_imag = elemental[:, 1]

    def contract(left, right):
        return jnp.einsum("ekn,snc->eskc", left, right, preferred_element_type=jnp.float32)

    prod_real = contract(el_real, tau_real) - contract(el_imag, tau_imag)
    prod_imag = contract(el_real, tau_imag) + contract(el_imag, tau_real)
    rows = prod_real.shape[0] * 4
    prod_real = prod_real.reshape(rows, -1)
    prod_imag = prod_imag.reshape(rows, -1)
    ops = w_real.shape[0]
    mix_real = w_real.reshape(ops * 4, rows)
    mix_imag = w_imag.reshape(ops * 4, rows)
    x_real = high_dot(mix_real, prod_real) - high_dot(mix_imag, prod_imag)
    x_imag = high_dot(mix_real, prod_imag) + high_dot(mix_imag, prod_real)
    return x_real.reshape(ops, -1).astype(jnp.bfloat16), x_imag.reshape(ops, -1).astype(jnp.bfloat16)


def source_side(peramb, elemental, w_real, w_imag, gamma_five):
    nev = elemental.shape[-1]
    nelem = elemental.shape[0]
    tau_real = peramb[0]
    tau_imag = peramb[1]
    el_real = elemental[:, 0]
    el_imag = elemental[:, 1]

    def contract(left, right):
        return jnp.einsum("fkm,snrm->fsnrk", left, right, preferred_element_type=jnp.float32)

    signs = (gamma_five[:, None, None, None] * gamma_five[None, None, :, None]).astype(jnp.float32)
    q_real = (contract(el_real, tau_real) + contract(el_imag, tau_imag)) * signs
    q_imag = (contract(el_imag, tau_real) - contract(el_real, tau_imag)) * signs
    q_real = q_real.reshape(nelem, 4 * nev, 4, nev)
    q_imag = q_imag.reshape(nelem, 4 * nev, 4, nev)

    def mixing(left, right):
        return jnp.einsum("jrfp,fapm->jarm", left, right, precision=lax.Precision.HIGHEST, preferred_element_type=jnp.float32)

    y_real = mixing(w_real, q_real) - mixing(w_imag, q_imag)
    y_imag = mixing(w_real, q_imag) + mixing(w_imag, q_real)
    ops = w_real.shape[0]
    return y_real.reshape(ops, -1).astype(jnp.bfloat16), y_imag.reshape(ops, -1).astype(jnp.bfloat16)


def trace_pair(x_parts, y_parts):
    x_real = x_parts[0].astype(jnp.float32)
    x_imag = x_parts[1].astype(jnp.float32)
    y_real = y_parts[0].astype(jnp.float32)
    y_imag = y_parts[1].astype(jnp.float32)

    def inner(left, right):
        return lax.dot_general(left, right, (((1,), (1,)), ((), ())), preferred_element_type=jnp.float32)

    c_real = inner(x_real, y_real) - inner(x_imag, y_imag)
    c_imag = inner(x_real, y_imag) + inner(x_imag, y_real)
    return jnp.stack([c_real, c_imag], axis=-1)


def reference(perambulators, elementals, gamma_codes, momenta, displacements, sink_times):
    w_real, w_imag, gamma_five = operator_weights(gamma_codes, momenta, displacements, NMOM * NDISP, NDISP)

    def pair_result(pair_index):
        src_time = pair_index // NT
        slot_index = pair_index % NT
        sink_time = lax.dynamic_index_in_dim(sink_times, slot_index, 0, keepdims=False).astype(jnp.int32)
        peramb = lax.dynamic_index_in_dim(lax.dynamic_index_in_dim(perambulators, src_time, 0, keepdims=False), slot_index, 0, keepdims=False).astype(jnp.float32)
        sink_elem = lax.dynamic_index_in_dim(elementals, sink_time, 0, keepdims=False).astype(jnp.float32)
        source_elem = lax.dynamic_index_in_dim(elementals, src_time, 0, keepdims=False).astype(jnp.float32)
        x_parts = sink_side(peramb, sink_elem, w_real, w_imag)
        y_parts = source_side(peramb, source_elem, w_real, w_imag, gamma_five)
        return trace_pair(x_parts, y_parts)

    traces = lax.map(pair_result, jnp.arange(NT * NT, dtype=jnp.int32)).reshape(NT, NT, OPS, OPS, 2)
    positions = jnp.arange(NT, dtype=jnp.int32)
    inverse = jnp.sum(positions[None, :] * (sink_times[None, :] == positions[:, None]).astype(jnp.int32), axis=1).astype(jnp.int32)
    mirrored = traces[sink_times[None, :], inverse[:, None]]
    mirrored = jnp.swapaxes(mirrored, 2, 3)
    return 0.5 * (traces + mirrored)
```

```python
import jax
import jax.numpy as jnp
import numpy as np
from jax import lax
from jax.experimental import pallas as pl
from jax.experimental.pallas import tpu as pltpu
from jax.sharding import PartitionSpec as P

NDISP = 2
NEV = 128
OPS = 8
BOTH = ("src", "snk")
HIGH = lax.Precision.HIGHEST


def off_diagonal(upper, lower):
    return np.array(
        [
            [0, 0, upper[0, 0], upper[0, 1]],
            [0, 0, upper[1, 0], upper[1, 1]],
            [lower[0, 0], lower[0, 1], 0, 0],
            [lower[1, 0], lower[1, 1], 0, 0],
        ],
        dtype=complex,
    )


def gamma_tables():
    paulis = [
        np.array([[0, 1], [1, 0]], dtype=complex),
        np.array([[0, -1j], [1j, 0]], dtype=complex),
        np.array([[1, 0], [0, -1]], dtype=complex),
    ]
    identity = np.eye(2, dtype=complex)
    gammas = [off_diagonal(-1j * matrix, 1j * matrix) for matrix in paulis]
    gammas.append(off_diagonal(identity, identity))
    gamma_table = []
    for gamma_code in range(16):
        product = np.eye(4, dtype=complex)
        for bit_index in range(4):
            if gamma_code >> bit_index & 1:
                product = product @ gammas[bit_index]
        gamma_table.append(product)
    return np.stack(gamma_table)


def phase_table():
    table = gamma_tables()
    numbers = []
    for code in range(16):
        rows = [int(np.argmax(np.abs(table[code][:, col]))) for col in range(4)]
        phases = [
            int(np.round(np.angle(table[code][rows[col], col]) / (np.pi / 2))) % 4
            for col in range(4)
        ]
        numbers += phases + [rows[0]]
    return np.array(numbers, np.int32)


def weights_kernel(code_ref, table_ref, wr_ref, wi_ref):
    row = lax.broadcasted_iota(jnp.int32, (256, NEV), 0)
    row_a, row_b, row_i = row >> 5 & 3, row >> 3 & 3, row & 7
    row_phase, row_xor = row >> 7, jnp.zeros_like(row)
    col = lax.broadcasted_iota(jnp.int32, (8, 256), 1)
    col_j, col_a, col_b = col >> 5, col >> 2 & 3, col & 3
    col_phase = (col >> 4 & 1) + 2 * ((col_a >> 1) ^ (col_b >> 1))
    col_xor = jnp.zeros_like(col)
    for op in range(OPS):
        base = code_ref[op] * 5
        row_xor = jnp.where(row_i == op, table_ref[base + 4], row_xor)
        col_xor = jnp.where(col_j == op, table_ref[base + 4], col_xor)
        for spin in range(4):
            phase = table_ref[base + spin]
            row_phase += jnp.where((row_i == op) & (row_a == spin), phase, 0)
            col_phase += jnp.where((col_j == op) & (col_b == spin), phase, 0)
    for half in range(2):
        lanes = slice(half * NEV, (half + 1) * NEV)
        shape = (256, NEV)
        c_phase = jnp.broadcast_to(col_phase[:1, lanes], shape)
        c_xor = jnp.broadcast_to(col_xor[:1, lanes], shape)
        c_a = jnp.broadcast_to(col_a[:1, lanes], shape)
        c_b = jnp.broadcast_to(col_b[:1, lanes], shape)
        kept = ((row_a ^ c_a) == row_xor) & ((row_b ^ c_b) == c_xor)
        phase = (row_phase + c_phase) & 3
        size = jnp.where(kept, 1.0, 0.0)
        sign = jnp.where(phase >= 2, -size, size)
        odd = (phase & 1) == 1
        wr_ref[:, lanes] = jnp.where(odd, 0.0, sign)
        wi_ref[:, lanes] = jnp.where(odd, sign, 0.0)


def mixing_weights(gamma_codes):
    smem = pl.BlockSpec(memory_space=pltpu.SMEM)
    vmem = pl.BlockSpec(memory_space=pltpu.VMEM)
    return pl.pallas_call(
        weights_kernel,
        out_shape=[jax.ShapeDtypeStruct((256, 256), jnp.float32)] * 2,
        in_specs=[smem, smem],
        out_specs=[vmem, vmem],
        name="mixing_weights",
    )(gamma_codes, jnp.asarray(phase_table()))


def rows_kernel(place_ref, elem_ref, el_ref, out_ref):
    parts = []
    for i in range(OPS):
        e = elem_ref[i]
        parts.append(
            jnp.concatenate(
                [el_ref[e, 0].astype(jnp.float32), el_ref[e, 1].astype(jnp.float32)], axis=1
            )
        )
    out_ref[...] = jnp.swapaxes(jnp.stack(parts), 0, 1).astype(jnp.bfloat16)


def operator_rows(place, elem_index, elemental):
    return pl.pallas_call(
        rows_kernel,
        out_shape=jax.ShapeDtypeStruct((16, OPS, 2 * NEV), jnp.bfloat16),
        grid_spec=pltpu.PrefetchScalarGridSpec(
            num_scalar_prefetch=2,
            grid=(1,),
            in_specs=[pl.BlockSpec((8, 2, 16, NEV), lambda g, k, e: (0, 0, k[0], 0))],
            out_specs=pl.BlockSpec((16, OPS, 2 * NEV), lambda g, k, e: (0, 0, 0)),
        ),
        name="operator_rows",
    )(place, elem_index, elemental)


def dot_nt(left, right):
    return lax.dot_general(
        left, right, (((1,), (1,)), ((), ())), preferred_element_type=jnp.float32
    )


def slot_rows_kernel(times_ref, spread_ref, *refs):
    out_refs, (held_ref, sem) = refs[:-2], refs[-2:]
    slots = len(out_refs)
    for slot in range(slots):
        for k in range(8):
            held_ref[slot, k] = spread_ref[times_ref[k * slots + slot]]
    copies = [
        pltpu.make_async_copy(held_ref.at[slot], out_refs[slot].at[s], sem.at[slot, s])
        for slot in range(slots)
        for s in range(16)
    ]
    for copy in copies:
        copy.start()
    for copy in copies:
        copy.wait()


def slot_rows(sink_times, spread, slots):
    return pl.pallas_call(
        slot_rows_kernel,
        out_shape=[jax.ShapeDtypeStruct((16, 8, OPS, 2 * NEV), jnp.bfloat16)] * slots,
        in_specs=[
            pl.BlockSpec(memory_space=pltpu.SMEM),
            pl.BlockSpec(memory_space=pltpu.VMEM),
        ],
        out_specs=[pl.BlockSpec(memory_space=pl.ANY)] * slots,
        scratch_shapes=[
            pltpu.VMEM((slots, 8, OPS, 2 * NEV), jnp.bfloat16),
            pltpu.SemaphoreType.DMA((slots, 16)),
        ],
        name="slot_rows",
    )(sink_times, spread)


def source_kernel(elem_ref, tau_ref, el_ref, after_ref, out_ref):
    count = out_ref.shape[0]
    lhs = jnp.concatenate([tau_ref[0, 0], tau_ref[0, 1]], axis=1)
    for j in range(OPS):
        e = elem_ref[j]
        b_real, b_imag = el_ref[e, 0], el_ref[e, 1]
        weight = jnp.concatenate(
            [
                jnp.concatenate([b_real, b_imag], axis=1),
                jnp.concatenate([b_imag, -b_real], axis=1),
            ],
            axis=0,
        )
        result = dot_nt(lhs, weight)
        for c in range(2):
            row = (2 * j + c) * 16
            part = result[:, c * NEV : (c + 1) * NEV].reshape(count, 16, NEV)
            out_ref[:, row : row + 16, :] = part.astype(jnp.bfloat16)


def source_side(slot, elem_index, tau_rows, elemental, after):
    block = 32
    return pl.pallas_call(
        source_kernel,
        out_shape=jax.ShapeDtypeStruct((NEV, 256, NEV), jnp.bfloat16),
        grid_spec=pltpu.PrefetchScalarGridSpec(
            num_scalar_prefetch=1,
            grid=(NEV // block,),
            in_specs=[
                pl.BlockSpec((1, 2, block * 16, NEV), lambda h, s: (slot, 0, h, 0)),
                pl.BlockSpec((8, 2, NEV, NEV), lambda h, s: (0, 0, 0, 0)),
                pl.BlockSpec(memory_space=pl.ANY),
            ],
            out_specs=pl.BlockSpec((block, 256, NEV), lambda h, s: (h, 0, 0)),
        ),
        compiler_params=pltpu.CompilerParams(vmem_limit_bytes=32 * 1024 * 1024),
        cost_estimate=pl.CostEstimate(
            flops=2 * 2048 * 256 * 2048, bytes_accessed=9 * 1024 * 1024, transcendentals=0
        ),
        name="source_side",
    )(elem_index, tau_rows, elemental, after)


CHUNKS = 8


def sink_kernel(final, *refs):
    if final:
        times_ref, *refs = refs
        el_ref, tau_ref, q_hbm, wr_ref, wi_ref, first_ref, *refs = refs
        out_ref, sent_ref, q_ref, p_ref, acc_ref, sems = refs
    else:
        el_ref, tau_ref, q_hbm, wr_ref, wi_ref, out_ref, q_ref, p_ref, acc_ref, sems = refs
    size = NEV // CHUNKS

    def copy_of(h):
        part = pl.ds(h * size, size)
        return pltpu.make_async_copy(q_hbm.at[part], q_ref.at[part], sems.at[h])

    for h in range(CHUNKS):
        copy_of(h).start()
    left = el_ref[...]

    def product(g, _):
        for c in range(2):
            tiles = []
            for ab in range(2):
                t_real, t_imag = tau_ref[0, 0, 2 * g + ab], tau_ref[0, 1, 2 * g + ab]
                upper, lower = (t_real, -t_imag) if c == 0 else (t_imag, t_real)
                tiles.append(jnp.concatenate([upper, lower], axis=0))
            result = jnp.dot(
                left, jnp.concatenate(tiles, axis=1), preferred_element_type=jnp.float32
            )
            both = jnp.concatenate(
                [
                    result[:, :NEV].reshape(NEV, 8, NEV),
                    result[:, NEV:].reshape(NEV, 8, NEV),
                ],
                axis=1,
            ).astype(jnp.bfloat16)
            p_ref[:, pl.ds(pl.multiple_of(c * 128 + g * 16, 16), 16), :] = both
        return 0

    lax.fori_loop(0, 8, product, 0)
    acc_ref[...] = jnp.zeros_like(acc_ref)

    def trace(h, _):
        copy_of(h).wait()
        lhs = jnp.concatenate([p_ref[h * size + u] for u in range(size)], axis=1)
        rhs = jnp.concatenate([q_ref[h * size + u] for u in range(size)], axis=1)
        acc_ref[...] += dot_nt(lhs, rhs)
        return 0

    lax.fori_loop(0, CHUNKS, trace, 0)
    sums = []
    for w_ref in (wr_ref, wi_ref):
        total = acc_ref[0:8, :] * w_ref[0:8, :]
        for r in range(1, 32):
            total = total + acc_ref[8 * r : 8 * r + 8, :] * w_ref[8 * r : 8 * r + 8, :]
        sums.append(total)
    col = lax.broadcasted_iota(jnp.int32, (256, NEV), 0) // 32
    lane = lax.broadcasted_iota(jnp.int32, (256, NEV), 1)
    lane8 = lax.broadcasted_iota(jnp.int32, (8, NEV), 1)
    row8 = lax.broadcasted_iota(jnp.int32, (8, NEV), 0)
    rows = []
    for j_at, i_at in ((2, 16), (16, 2)):
        total = 0.0
        for c in range(2):
            spread = ((lane // j_at % 8 == col) & (lane % 2 == c)).astype(jnp.float32)
            total = total + jnp.dot(
                sums[c], spread, precision=HIGH, preferred_element_type=jnp.float32
            )
        kept = jnp.where(lane8 // i_at % 8 == row8, total, 0.0)
        rows.append(jnp.sum(kept, axis=0, keepdims=True))
    out_ref[...] = jnp.where(row8 == 0, rows[0], rows[1])
    if final:
        to_time = lax.broadcasted_iota(jnp.int32, (128, NEV), 0) >> 3
        sent = jnp.where(to_time == times_ref[0], first_ref[1:2, :], 0.0)
        sent_ref[...] = jnp.where(to_time == times_ref[1], rows[1], sent)


def sink_side(slot, elemental, tau_cols, q_rows, weights, slot_times=None, first=None):
    vmem = pl.BlockSpec(memory_space=pltpu.VMEM)
    final = first is not None
    out_shape = [jax.ShapeDtypeStruct((8, NEV), jnp.float32)]
    in_specs = [
        vmem,
        pl.BlockSpec((1, 2, 16, NEV, NEV), lambda g: (slot, 0, 0, 0, 0)),
        pl.BlockSpec(memory_space=pl.ANY),
        vmem,
        vmem,
    ]
    operands = [elemental, tau_cols, q_rows, *weights]
    if final:
        out_shape.append(jax.ShapeDtypeStruct((128, NEV), jnp.float32))
        in_specs = [pl.BlockSpec(memory_space=pltpu.SMEM)] + in_specs + [vmem]
        operands = [slot_times] + operands + [first]
    return pl.pallas_call(
        lambda *refs: sink_kernel(final, *refs),
        grid=(1,),
        out_shape=out_shape,
        in_specs=in_specs,
        out_specs=[vmem] * len(out_shape),
        scratch_shapes=[
            pltpu.VMEM((NEV, 256, NEV), jnp.bfloat16),
            pltpu.VMEM((NEV, 256, NEV), jnp.bfloat16),
            pltpu.VMEM((256, 256), jnp.float32),
            pltpu.SemaphoreType.DMA((CHUNKS,)),
        ],
        compiler_params=pltpu.CompilerParams(vmem_limit_bytes=48 * 1024 * 1024),
        cost_estimate=pl.CostEstimate(
            flops=2 * 2 * 2048 * 256 * 2048, bytes_accessed=10 * 1024 * 1024, transcendentals=0
        ),
        name="sink_side",
    )(*operands)


def average_kernel(times_ref, place_ref, arrived_ref, *refs):
    own_refs, out_ref = refs[:-1], refs[-1]
    slots = len(own_refs)
    here = jnp.int32(0)
    for slot in range(times_ref.shape[0]):
        here = here + jnp.where(times_ref[slot] == place_ref[0], slot, 0)
    lane = lax.broadcasted_iota(jnp.int32, (16, NEV), 1)
    row = lax.broadcasted_iota(jnp.int32, (16, NEV), 0)
    kept = ((lane >> 4) == (row >> 1)) & ((lane & 1) == (row & 1))
    from_lane = lax.broadcasted_iota(jnp.int32, (NEV, NEV), 0) >> 1 & 7
    to_lane = lax.broadcasted_iota(jnp.int32, (NEV, NEV), 1)
    fold = (from_lane == to_lane).astype(jnp.float32)
    for slot in range(slots):
        at = times_ref[place_ref[1] * slots + slot] * 8 + here // slots
        mean = 0.5 * (own_refs[slot][0:1, :] + arrived_ref[at])
        spread = jnp.where(kept, jnp.broadcast_to(mean, (16, NEV)), 0.0)
        folded = jnp.dot(spread, fold, precision=HIGH, preferred_element_type=jnp.float32)
        for i in range(OPS):
            out_ref[slot, i] = folded[2 * i : 2 * i + 2, :OPS]


def average(sink_times, place, arrived, own):
    smem = pl.BlockSpec(memory_space=pltpu.SMEM)
    vmem = pl.BlockSpec(memory_space=pltpu.VMEM)
    return pl.pallas_call(
        average_kernel,
        out_shape=jax.ShapeDtypeStruct((len(own), OPS, 2, OPS), jnp.float32),
        in_specs=[smem, smem] + [vmem] * (1 + len(own)),
        out_specs=vmem,
        name="average",
    )(sink_times, place, arrived, *own)


def shards(perambulators, elementals, gamma_codes, momenta, displacements, sink_times):
    slots = perambulators.shape[1]
    src_index = lax.axis_index("src")
    snk_index = lax.axis_index("snk")
    place = jnp.stack([src_index, snk_index]).astype(jnp.int32)
    elem_index = momenta * NDISP + displacements
    source_elem = elementals[0]

    rows = operator_rows(place[1:], elem_index, source_elem)
    spread = lax.all_to_all(rows, "src", 0, 0, tiled=True)
    sent = slot_rows(sink_times, spread, slots)
    sink_rows = [
        lax.all_to_all(part.reshape(128, OPS, 2 * NEV), BOTH, 0, 0, tiled=True) for part in sent
    ]
    tau_rows = (
        perambulators[0]
        .reshape(slots, 2, 4, 8, 16, 4, NEV)
        .transpose(0, 1, 4, 3, 2, 5, 6)
        .reshape(slots, 2, 2048, NEV)
    )
    tau_cols = perambulators[0].transpose(0, 1, 2, 4, 3, 5).reshape(slots, 2, 16, NEV, NEV)
    weights = mixing_weights(gamma_codes)
    slot_times = lax.dynamic_slice_in_dim(sink_times, snk_index * slots, slots)
    q_rows = [
        source_side(slot, elem_index, tau_rows, source_elem, sent[-1]) for slot in range(slots)
    ]
    elems = [part.reshape(1024, 2 * NEV) for part in sink_rows]
    (first,) = sink_side(0, elems[0], tau_cols, q_rows[0], weights)
    second, mirror = sink_side(1, elems[1], tau_cols, q_rows[1], weights, slot_times, first)
    arrived = lax.all_to_all(mirror[:, None], BOTH, 0, 0, tiled=True)
    result = average(sink_times, place, arrived, (first, second))
    return result.transpose(0, 1, 3, 2)[None]


def solution(mesh):
    in_specs = (
        P("src", "snk", None, None, None, None, None),
        P("src", None, None, None, None),
        P(),
        P(),
        P(),
        P(),
    )
    out_specs = P("src", "snk", None, None, None)
    return jax.shard_map(shards, mesh=mesh, in_specs=in_specs, out_specs=out_specs, check_vma=False)
```

```python
import jax
import jax.numpy as jnp
import numpy as np
from jax import lax
from jax.experimental import pallas as pl
from jax.experimental.pallas import tpu as pltpu
from jax.sharding import PartitionSpec as P

NDISP = 2
NEV = 128
OPS = 8
BOTH = ("src", "snk")
HIGH = lax.Precision.HIGHEST
VMEM_LIMIT = 56 * 1024 * 1024


def off_diagonal(upper, lower):
    return np.array(
        [
            [0, 0, upper[0, 0], upper[0, 1]],
            [0, 0, upper[1, 0], upper[1, 1]],
            [lower[0, 0], lower[0, 1], 0, 0],
            [lower[1, 0], lower[1, 1], 0, 0],
        ],
        dtype=complex,
    )


def gamma_tables():
    paulis = [
        np.array([[0, 1], [1, 0]], dtype=complex),
        np.array([[0, -1j], [1j, 0]], dtype=complex),
        np.array([[1, 0], [0, -1]], dtype=complex),
    ]
    identity = np.eye(2, dtype=complex)
    gammas = [off_diagonal(-1j * matrix, 1j * matrix) for matrix in paulis]
    gammas.append(off_diagonal(identity, identity))
    gamma_table = []
    for gamma_code in range(16):
        product = np.eye(4, dtype=complex)
        for bit_index in range(4):
            if gamma_code >> bit_index & 1:
                product = product @ gammas[bit_index]
        gamma_table.append(product)
    return np.stack(gamma_table)


def phase_table():
    table = gamma_tables()
    numbers = []
    for code in range(16):
        rows = [int(np.argmax(np.abs(table[code][:, col]))) for col in range(4)]
        phases = [
            int(np.round(np.angle(table[code][rows[col], col]) / (np.pi / 2))) % 4
            for col in range(4)
        ]
        numbers += phases + [rows[0]]
    return np.array(numbers, np.int32)


def weights_kernel(code_ref, table_ref, wr_ref, wi_ref):
    row = lax.broadcasted_iota(jnp.int32, (256, NEV), 0)
    row_a, row_b, row_i = row >> 5 & 3, row >> 3 & 3, row & 7
    row_phase, row_xor = row >> 7, jnp.zeros_like(row)
    col = lax.broadcasted_iota(jnp.int32, (8, 256), 1)
    col_j, col_a, col_b = col >> 5, col >> 2 & 3, col & 3
    col_phase = (col >> 4 & 1) + 2 * ((col_a >> 1) ^ (col_b >> 1))
    col_xor = jnp.zeros_like(col)
    for op in range(OPS):
        base = code_ref[op] * 5
        row_xor = jnp.where(row_i == op, table_ref[base + 4], row_xor)
        col_xor = jnp.where(col_j == op, table_ref[base + 4], col_xor)
        for spin in range(4):
            phase = table_ref[base + spin]
            row_phase += jnp.where((row_i == op) & (row_a == spin), phase, 0)
            col_phase += jnp.where((col_j == op) & (col_b == spin), phase, 0)
    for half in range(2):
        lanes = slice(half * NEV, (half + 1) * NEV)
        shape = (256, NEV)
        c_phase = jnp.broadcast_to(col_phase[:1, lanes], shape)
        c_xor = jnp.broadcast_to(col_xor[:1, lanes], shape)
        c_a = jnp.broadcast_to(col_a[:1, lanes], shape)
        c_b = jnp.broadcast_to(col_b[:1, lanes], shape)
        kept = ((row_a ^ c_a) == row_xor) & ((row_b ^ c_b) == c_xor)
        phase = (row_phase + c_phase) & 3
        size = jnp.where(kept, 1.0, 0.0)
        sign = jnp.where(phase >= 2, -size, size)
        odd = (phase & 1) == 1
        wr_ref[:, lanes] = jnp.where(odd, 0.0, sign)
        wi_ref[:, lanes] = jnp.where(odd, sign, 0.0)


def mixing_weights(gamma_codes):
    smem = pl.BlockSpec(memory_space=pltpu.SMEM)
    vmem = pl.BlockSpec(memory_space=pltpu.VMEM)
    return pl.pallas_call(
        weights_kernel,
        out_shape=[jax.ShapeDtypeStruct((256, 256), jnp.float32)] * 2,
        in_specs=[smem, smem],
        out_specs=[vmem, vmem],
        name="mixing_weights",
    )(gamma_codes, jnp.asarray(phase_table()))


def rows_kernel(place_ref, momenta_ref, displacements_ref, el_ref, out_ref):
    parts = []
    for i in range(OPS):
        e = momenta_ref[i] * NDISP + displacements_ref[i]
        parts.append(
            jnp.concatenate(
                [el_ref[e, 0].astype(jnp.float32), el_ref[e, 1].astype(jnp.float32)], axis=1
            )
        )
    out_ref[...] = jnp.swapaxes(jnp.stack(parts), 0, 1).astype(jnp.bfloat16)


def operator_rows(place, momenta, displacements, elemental):
    return pl.pallas_call(
        rows_kernel,
        out_shape=jax.ShapeDtypeStruct((16, OPS, 2 * NEV), jnp.bfloat16),
        grid_spec=pltpu.PrefetchScalarGridSpec(
            num_scalar_prefetch=3,
            grid=(1,),
            in_specs=[pl.BlockSpec((8, 2, 16, NEV), lambda g, k, m, d: (0, 0, k[0], 0))],
            out_specs=pl.BlockSpec((16, OPS, 2 * NEV), lambda g, k, m, d: (0, 0, 0)),
        ),
        name="operator_rows",
    )(place, momenta, displacements, elemental)


def dot_nt(left, right):
    return lax.dot_general(
        left, right, (((1,), (1,)), ((), ())), preferred_element_type=jnp.float32
    )


def slot_rows_kernel(times_ref, spread_ref, out_ref, held_ref, sem):
    for slot in range(held_ref.shape[0]):
        held_ref[slot] = spread_ref[times_ref[slot]]
    copies = [
        pltpu.make_async_copy(held_ref, out_ref.at[s], sem.at[s]) for s in range(16)
    ]
    for copy in copies:
        copy.start()
    for copy in copies:
        copy.wait()


def slot_rows(sink_times, spread):
    total = sink_times.shape[0]
    return pl.pallas_call(
        slot_rows_kernel,
        out_shape=jax.ShapeDtypeStruct((16, total, OPS, 2 * NEV), jnp.bfloat16),
        in_specs=[
            pl.BlockSpec(memory_space=pltpu.SMEM),
            pl.BlockSpec(memory_space=pltpu.VMEM),
        ],
        out_specs=pl.BlockSpec(memory_space=pl.ANY),
        scratch_shapes=[
            pltpu.VMEM((total, OPS, 2 * NEV), jnp.bfloat16),
            pltpu.SemaphoreType.DMA((16,)),
        ],
        name="slot_rows",
    )(sink_times, spread)


def source_kernel(momenta_ref, displacements_ref, tau_ref, el_ref, after_ref, *refs):
    out_ref, held_ref, sems = refs

    def copy_of(slot, part):
        rows = slice(64 * part, 64 * (part + 1))
        return pltpu.make_async_copy(
            held_ref.at[slot, :, rows], out_ref.at[slot, :, rows], sems.at[slot, part]
        )

    def product(slot, _):
        lhs = jnp.concatenate([tau_ref[slot, 0], tau_ref[slot, 1]], axis=1)
        for j in range(OPS):
            e = momenta_ref[j] * NDISP + displacements_ref[j]
            b_real, b_imag = el_ref[e, 0], el_ref[e, 1]
            weight = jnp.concatenate(
                [
                    jnp.concatenate([b_real, b_imag], axis=1),
                    jnp.concatenate([b_imag, -b_real], axis=1),
                ],
                axis=0,
            )
            result = dot_nt(lhs, weight)
            for c in range(2):
                row = (2 * j + c) * 16
                part = result[:, c * NEV : (c + 1) * NEV].reshape(NEV, 16, NEV)
                held_ref[slot, :, row : row + 16, :] = part.astype(jnp.bfloat16)
            if j % 2 == 1:
                copy_of(slot, j // 2).start()
        return 0

    lax.fori_loop(0, 2, product, 0)
    for slot in range(2):
        for part in range(4):
            copy_of(slot, part).wait()


def source_side(momenta, displacements, tau_rows, elemental, after):
    smem = pl.BlockSpec(memory_space=pltpu.SMEM)
    vmem = pl.BlockSpec(memory_space=pltpu.VMEM)
    hbm = pl.BlockSpec(memory_space=pltpu.HBM)
    return pl.pallas_call(
        source_kernel,
        out_shape=jax.ShapeDtypeStruct((2, NEV, 256, NEV), jnp.bfloat16),
        in_specs=[smem, smem, vmem, vmem, hbm],
        out_specs=hbm,
        scratch_shapes=[
            pltpu.VMEM((2, NEV, 256, NEV), jnp.bfloat16),
            pltpu.SemaphoreType.DMA((2, 4)),
        ],
        compiler_params=pltpu.CompilerParams(vmem_limit_bytes=VMEM_LIMIT),
        cost_estimate=pl.CostEstimate(
            flops=4 * 2048 * 256 * 2048, bytes_accessed=20 * 1024 * 1024, transcendentals=0
        ),
        name="source_side",
    )(momenta, displacements, tau_rows, elemental, after)


def sink_kernel(times_ref, place_ref, el_hbm, tau_hbm, wr_ref, wi_ref, q_hbm, *refs):
    own_ref, sent_ref, el_ref, left_ref, tau_ref, p_ref, q_ref, acc_ref, sems = refs
    el_copy = pltpu.make_async_copy(el_hbm, el_ref, sems.at[4])

    def tau_copy(slot):
        return pltpu.make_async_copy(tau_hbm.at[slot], tau_ref.at[slot], sems.at[slot])

    def q_copy(slot):
        return pltpu.make_async_copy(q_hbm.at[slot], q_ref.at[slot], sems.at[2 + slot])

    el_copy.start()
    for copy in (tau_copy, q_copy):
        for slot in range(2):
            copy(slot).start()
    el_copy.wait()
    both_slots = el_ref[...].astype(jnp.float32).reshape(NEV, 2, OPS, 2 * NEV)
    for slot in range(2):
        left = both_slots[:, slot].reshape(1024, 2 * NEV)
        left_ref[slot] = left.astype(jnp.bfloat16)

    def product(slot, _):
        tau_copy(slot).wait()
        for c in range(2):
            for g in range(8):
                tiles = []
                for ab in range(2):
                    t_real, t_imag = tau_ref[slot, 0, 2 * g + ab], tau_ref[slot, 1, 2 * g + ab]
                    upper, lower = (t_real, -t_imag) if c == 0 else (t_imag, t_real)
                    tiles.append(jnp.concatenate([upper, lower], axis=0))
                result = jnp.dot(
                    left_ref[slot],
                    jnp.concatenate(tiles, axis=1),
                    preferred_element_type=jnp.float32,
                )
                both = jnp.concatenate(
                    [
                        result[:, :NEV].reshape(NEV, OPS, NEV),
                        result[:, NEV:].reshape(NEV, OPS, NEV),
                    ],
                    axis=1,
                )
                row = c * 128 + g * 16
                p_ref[slot, :, row : row + 16, :] = both.astype(jnp.bfloat16)
        return 0

    lax.fori_loop(0, 2, product, 0)

    col = lax.broadcasted_iota(jnp.int32, (256, NEV), 0) >> 5
    lane = lax.broadcasted_iota(jnp.int32, (256, NEV), 1)
    lane8 = lax.broadcasted_iota(jnp.int32, (8, NEV), 1)
    row8 = lax.broadcasted_iota(jnp.int32, (8, NEV), 0)
    to_time = lax.broadcasted_iota(jnp.int32, (128, NEV), 0) >> 3
    sent_ref[...] = jnp.zeros((128, NEV), jnp.float32)

    def trace(slot, _):
        q_copy(slot).wait()
        acc_ref[...] = jnp.zeros_like(acc_ref)
        for h in range(8):
            lhs = jnp.concatenate([p_ref[slot, 16 * h + n] for n in range(16)], axis=1)
            rhs = jnp.concatenate([q_ref[slot, 16 * h + n] for n in range(16)], axis=1)
            acc_ref[...] += dot_nt(lhs, rhs)
        sums = []
        for w_ref in (wr_ref, wi_ref):
            total = acc_ref[0:8, :] * w_ref[0:8, :]
            for r in range(1, 32):
                total = total + acc_ref[8 * r : 8 * r + 8, :] * w_ref[8 * r : 8 * r + 8, :]
            sums.append(total)
        rows = []
        for j_at, i_at in ((1, 4), (4, 1)):
            total = 0.0
            for c in range(2):
                spread = ((lane >> j_at & 7) == col) & ((lane & 1) == c)
                total = total + jnp.dot(
                    sums[c],
                    spread.astype(jnp.float32),
                    precision=HIGH,
                    preferred_element_type=jnp.float32,
                )
            kept = jnp.where((lane8 >> i_at & 7) == row8, total, 0.0)
            rows.append(jnp.sum(kept, axis=0, keepdims=True))
        own_ref[slot] = jnp.broadcast_to(rows[0], (8, NEV))
        here = to_time == times_ref[place_ref[1] * 2 + slot]
        sent_ref[...] = jnp.where(here, rows[1], sent_ref[...])
        return 0

    lax.fori_loop(0, 2, trace, 0)


def sink_side(sink_times, place, elemental, tau_cols, weights, q_rows):
    smem = pl.BlockSpec(memory_space=pltpu.SMEM)
    vmem = pl.BlockSpec(memory_space=pltpu.VMEM)
    hbm = pl.BlockSpec(memory_space=pltpu.HBM)
    return pl.pallas_call(
        sink_kernel,
        out_shape=[
            jax.ShapeDtypeStruct((2, 8, NEV), jnp.float32),
            jax.ShapeDtypeStruct((128, NEV), jnp.float32),
        ],
        in_specs=[smem, smem, hbm, hbm, vmem, vmem, hbm],
        out_specs=[vmem] * 2,
        scratch_shapes=[
            pltpu.VMEM((2048, 2 * NEV), jnp.bfloat16),
            pltpu.VMEM((2, 1024, 2 * NEV), jnp.bfloat16),
            pltpu.VMEM((2, 2, 16, NEV, NEV), jnp.bfloat16),
            pltpu.VMEM((2, NEV, 256, NEV), jnp.bfloat16),
            pltpu.VMEM((2, NEV, 256, NEV), jnp.bfloat16),
            pltpu.VMEM((256, 256), jnp.float32),
            pltpu.SemaphoreType.DMA((5,)),
        ],
        compiler_params=pltpu.CompilerParams(vmem_limit_bytes=VMEM_LIMIT),
        cost_estimate=pl.CostEstimate(
            flops=8 * 2048 * 256 * 2048, bytes_accessed=20 * 1024 * 1024, transcendentals=0
        ),
        name="sink_side",
    )(sink_times, place, elemental, tau_cols, *weights, q_rows)


def average_kernel(times_ref, place_ref, arrived_ref, own_ref, out_ref):
    slots = own_ref.shape[0]
    here = jnp.int32(0)
    for slot in range(times_ref.shape[0]):
        here = here + jnp.where(times_ref[slot] == place_ref[0], slot, 0)
    lane = lax.broadcasted_iota(jnp.int32, (16, NEV), 1)
    row = lax.broadcasted_iota(jnp.int32, (16, NEV), 0)
    kept = ((lane >> 4) == (row >> 1)) & ((lane & 1) == (row & 1))
    from_lane = lax.broadcasted_iota(jnp.int32, (NEV, NEV), 0) >> 1 & 7
    to_lane = lax.broadcasted_iota(jnp.int32, (NEV, NEV), 1)
    fold = (from_lane == to_lane).astype(jnp.float32)
    for slot in range(slots):
        at = times_ref[place_ref[1] * slots + slot] * 8 + here // slots
        mean = 0.5 * (own_ref[slot, 0:1, :] + arrived_ref[at])
        spread = jnp.where(kept, jnp.broadcast_to(mean, (16, NEV)), 0.0)
        folded = jnp.dot(spread, fold, precision=HIGH, preferred_element_type=jnp.float32)
        for i in range(OPS):
            out_ref[slot, i] = folded[2 * i : 2 * i + 2, :OPS]


def average(sink_times, place, arrived, own):
    smem = pl.BlockSpec(memory_space=pltpu.SMEM)
    vmem = pl.BlockSpec(memory_space=pltpu.VMEM)
    return pl.pallas_call(
        average_kernel,
        out_shape=jax.ShapeDtypeStruct((own.shape[0], OPS, 2, OPS), jnp.float32),
        in_specs=[smem, smem] + [vmem, vmem],
        out_specs=vmem,
        name="average",
    )(sink_times, place, arrived, own)


def shards(perambulators, elementals, gamma_codes, momenta, displacements, sink_times):
    slots = perambulators.shape[1]
    src_index = lax.axis_index("src")
    snk_index = lax.axis_index("snk")
    place = jnp.stack([src_index, snk_index]).astype(jnp.int32)
    source_elem = elementals[0]

    rows = operator_rows(place[1:], momenta, displacements, source_elem)
    spread = lax.all_to_all(rows, "src", 0, 0, tiled=True)
    sent = slot_rows(sink_times, spread)
    sink_rows = lax.all_to_all(sent.reshape(128, slots * OPS, 2 * NEV), BOTH, 0, 0, tiled=True)
    sink_rows = sink_rows.reshape(2048, 2 * NEV)
    tau_rows = (
        perambulators[0]
        .reshape(slots, 2, 4, 8, 16, 4, NEV)
        .transpose(0, 1, 4, 3, 2, 5, 6)
        .reshape(slots, 2, 2048, NEV)
    )
    tau_cols = perambulators[0].transpose(0, 1, 2, 4, 3, 5).reshape(slots, 2, 16, NEV, NEV)
    weights = mixing_weights(gamma_codes)
    q_rows = source_side(momenta, displacements, tau_rows, source_elem, sent)
    own, mirror = sink_side(sink_times, place, sink_rows, tau_cols, weights, q_rows)
    arrived = lax.all_to_all(mirror[:, None], BOTH, 0, 0, tiled=True)
    result = average(sink_times, place, arrived, own)
    return result.transpose(0, 1, 3, 2)[None]


def solution(mesh):
    in_specs = (
        P("src", "snk", None, None, None, None, None),
        P("src", None, None, None, None),
        P(),
        P(),
        P(),
        P(),
    )
    out_specs = P("src", "snk", None, None, None)
    return jax.shard_map(shards, mesh=mesh, in_specs=in_specs, out_specs=out_specs, check_vma=False)
```

```python
import jax
import jax.numpy as jnp
import numpy as np
from jax import lax
from jax.experimental import pallas as pl
from jax.experimental.pallas import tpu as pltpu
from jax.sharding import PartitionSpec as P

NDISP = 2
NEV = 128
OPS = 8
BOTH = ("src", "snk")
HIGH = lax.Precision.HIGHEST
VMEM_LIMIT = 56 * 1024 * 1024


def off_diagonal(upper, lower):
    return np.array(
        [
            [0, 0, upper[0, 0], upper[0, 1]],
            [0, 0, upper[1, 0], upper[1, 1]],
            [lower[0, 0], lower[0, 1], 0, 0],
            [lower[1, 0], lower[1, 1], 0, 0],
        ],
        dtype=complex,
    )


def gamma_tables():
    paulis = [
        np.array([[0, 1], [1, 0]], dtype=complex),
        np.array([[0, -1j], [1j, 0]], dtype=complex),
        np.array([[1, 0], [0, -1]], dtype=complex),
    ]
    identity = np.eye(2, dtype=complex)
    gammas = [off_diagonal(-1j * matrix, 1j * matrix) for matrix in paulis]
    gammas.append(off_diagonal(identity, identity))
    gamma_table = []
    for gamma_code in range(16):
        product = np.eye(4, dtype=complex)
        for bit_index in range(4):
            if gamma_code >> bit_index & 1:
                product = product @ gammas[bit_index]
        gamma_table.append(product)
    return np.stack(gamma_table)


def phase_table():
    table = gamma_tables()
    numbers = []
    for code in range(16):
        rows = [int(np.argmax(np.abs(table[code][:, col]))) for col in range(4)]
        phases = [
            int(np.round(np.angle(table[code][rows[col], col]) / (np.pi / 2))) % 4
            for col in range(4)
        ]
        numbers += phases + [rows[0]]
    return np.array(numbers, np.int32)


def weights_kernel(code_ref, table_ref, w_ref):
    row = lax.broadcasted_iota(jnp.int32, (256, NEV), 0)
    row_a, row_b, row_i = row >> 5 & 3, row >> 3 & 3, row & 7
    row_phase, row_xor = row >> 7, jnp.zeros_like(row)
    col = lax.broadcasted_iota(jnp.int32, (8, 256), 1)
    col_j, col_a, col_b = col >> 5, col >> 2 & 3, col & 3
    col_phase = (col >> 4 & 1) + 2 * ((col_a >> 1) ^ (col_b >> 1))
    col_xor = jnp.zeros_like(col)
    for op in range(OPS):
        base = code_ref[op] * 5
        row_xor = jnp.where(row_i == op, table_ref[base + 4], row_xor)
        col_xor = jnp.where(col_j == op, table_ref[base + 4], col_xor)
        for spin in range(4):
            phase = table_ref[base + spin]
            row_phase += jnp.where((row_i == op) & (row_a == spin), phase, 0)
            col_phase += jnp.where((col_j == op) & (col_b == spin), phase, 0)
    for half in range(2):
        lanes = slice(half * NEV, (half + 1) * NEV)
        shape = (256, NEV)
        c_phase = jnp.broadcast_to(col_phase[:1, lanes], shape)
        c_xor = jnp.broadcast_to(col_xor[:1, lanes], shape)
        c_a = jnp.broadcast_to(col_a[:1, lanes], shape)
        c_b = jnp.broadcast_to(col_b[:1, lanes], shape)
        kept = ((row_a ^ c_a) == row_xor) & ((row_b ^ c_b) == c_xor)
        phase = (row_phase + c_phase) & 3
        size = jnp.where(kept, 1.0, 0.0)
        sign = jnp.where(phase >= 2, -size, size)
        odd = (phase & 1) == 1
        w_ref[0, :, lanes] = jnp.where(odd, 0.0, sign).astype(jnp.bfloat16)
        w_ref[1, :, lanes] = jnp.where(odd, sign, 0.0).astype(jnp.bfloat16)


def mixing_weights(gamma_codes):
    smem = pl.BlockSpec(memory_space=pltpu.SMEM)
    vmem = pl.BlockSpec(memory_space=pltpu.VMEM)
    return pl.pallas_call(
        weights_kernel,
        out_shape=jax.ShapeDtypeStruct((2, 256, 256), jnp.bfloat16),
        in_specs=[smem, smem],
        out_specs=vmem,
        name="mixing_weights",
    )(gamma_codes, jnp.asarray(phase_table()))


def dot_nt(left, right):
    return lax.dot_general(
        left, right, (((1,), (1,)), ((), ())), preferred_element_type=jnp.float32
    )


def slot_parts_kernel(times_ref, place_ref, spread_ref, *refs):
    out_ref, held_ref, sem = refs[-3:]
    for slot in range(2):
        held_ref[slot] = spread_ref[times_ref[place_ref[1] * 2 + slot]]
    copies = [pltpu.make_async_copy(held_ref, out_ref.at[s], sem.at[s]) for s in range(16)]
    for copy in copies:
        copy.start()
    for copy in copies:
        copy.wait()


def slot_parts(sink_times, place, spread, before):
    smem = pl.BlockSpec(memory_space=pltpu.SMEM)
    hbm = pl.BlockSpec(memory_space=pltpu.HBM)
    return pl.pallas_call(
        slot_parts_kernel,
        out_shape=jax.ShapeDtypeStruct((16, 2, NEV, NEV), jnp.bfloat16),
        in_specs=[smem, smem, pl.BlockSpec(memory_space=pltpu.VMEM)] + [hbm] * len(before),
        out_specs=hbm,
        scratch_shapes=[
            pltpu.VMEM((2, NEV, NEV), jnp.bfloat16),
            pltpu.SemaphoreType.DMA((16,)),
        ],
        name="slot_parts",
    )(sink_times, place, spread, *before)


def source_kernel(momenta_ref, displacements_ref, tau_ref, el_ref, *refs):
    out_ref, held_ref, sems = refs

    def copy_of(slot, part):
        rows = slice(64 * part, 64 * (part + 1))
        return pltpu.make_async_copy(
            held_ref.at[slot, :, rows], out_ref.at[slot, :, rows], sems.at[slot, part]
        )

    def product(slot, _):
        lhs = jnp.concatenate([tau_ref[slot, 0], tau_ref[slot, 1]], axis=1)
        for j in range(OPS):
            e = momenta_ref[j] * NDISP + displacements_ref[j]
            b_real, b_imag = el_ref[e, 0], el_ref[e, 1]
            weight = jnp.concatenate(
                [
                    jnp.concatenate([b_real, b_imag], axis=1),
                    jnp.concatenate([b_imag, -b_real], axis=1),
                ],
                axis=0,
            )
            result = dot_nt(lhs, weight)
            for c in range(2):
                row = (2 * j + c) * 16
                part = result[:, c * NEV : (c + 1) * NEV].reshape(NEV, 16, NEV)
                held_ref[slot, :, row : row + 16, :] = part.astype(jnp.bfloat16)
            if j % 2 == 1:
                copy_of(slot, j // 2).start()
        return 0

    lax.fori_loop(0, 2, product, 0)
    for slot in range(2):
        for part in range(4):
            copy_of(slot, part).wait()


def source_side(momenta, displacements, tau_rows, elemental):
    smem = pl.BlockSpec(memory_space=pltpu.SMEM)
    vmem = pl.BlockSpec(memory_space=pltpu.VMEM)
    hbm = pl.BlockSpec(memory_space=pltpu.HBM)
    return pl.pallas_call(
        source_kernel,
        out_shape=jax.ShapeDtypeStruct((2, NEV, 256, NEV), jnp.bfloat16),
        in_specs=[smem, smem, vmem, vmem],
        out_specs=hbm,
        scratch_shapes=[
            pltpu.VMEM((2, NEV, 256, NEV), jnp.bfloat16),
            pltpu.SemaphoreType.DMA((2, 4)),
        ],
        compiler_params=pltpu.CompilerParams(vmem_limit_bytes=VMEM_LIMIT),
        cost_estimate=pl.CostEstimate(
            flops=4 * 2048 * 256 * 2048, bytes_accessed=20 * 1024 * 1024, transcendentals=0
        ),
        name="source_side",
    )(momenta, displacements, tau_rows, elemental)


CHUNKS = 1


def sink_kernel(times_ref, place_ref, momenta_ref, displacements_ref, *refs):
    el_ref, tau_hbm, w_hbm, q_hbm, own_ref, sent_ref, *refs = refs
    left_ref, tau_ref, p_ref, q_ref, acc_ref, w_ref, load_sems, q_sems = refs
    size = NEV // CHUNKS

    def tau_copy(slot):
        return pltpu.make_async_copy(tau_hbm.at[slot], tau_ref.at[slot], load_sems.at[slot])

    w_copy = pltpu.make_async_copy(w_hbm, w_ref, load_sems.at[2])

    def q_copy(slot, h):
        part = pl.ds(h * size, size)
        return pltpu.make_async_copy(
            q_hbm.at[slot, part], q_ref.at[slot, part], q_sems.at[slot, h]
        )

    for slot in range(2):
        tau_copy(slot).start()
        for h in range(CHUNKS):
            q_copy(slot, h).start()
    w_copy.start()

    def product(slot, _):
        elems = [momenta_ref[i] * NDISP + displacements_ref[i] for i in range(OPS)]

        def arrange(block, _):
            at = pl.ds(pl.multiple_of(16 * block, 16), 16)
            parts = [
                jnp.concatenate([el_ref[2 * e + c, slot, at, :] for c in range(2)], axis=1)
                for e in elems
            ]
            rows = jnp.swapaxes(jnp.stack(parts).astype(jnp.float32), 0, 1)
            rows = rows.reshape(128, 2 * NEV).astype(jnp.bfloat16)
            left_ref[pl.ds(pl.multiple_of(128 * block, 128), 128), :] = rows
            return 0

        lax.fori_loop(0, 8, arrange, 0)
        tau_copy(slot).wait()
        for c in range(2):
            for g in range(8):
                tiles = []
                for ab in range(2):
                    t_real, t_imag = tau_ref[slot, 0, 2 * g + ab], tau_ref[slot, 1, 2 * g + ab]
                    upper, lower = (t_real, -t_imag) if c == 0 else (t_imag, t_real)
                    tiles.append(jnp.concatenate([upper, lower], axis=0))
                result = jnp.dot(
                    left_ref[...],
                    jnp.concatenate(tiles, axis=1),
                    preferred_element_type=jnp.float32,
                )
                both = jnp.concatenate(
                    [
                        result[:, :NEV].reshape(NEV, OPS, NEV),
                        result[:, NEV:].reshape(NEV, OPS, NEV),
                    ],
                    axis=1,
                )
                row = c * 128 + g * 16
                p_ref[slot, :, row : row + 16, :] = both.astype(jnp.bfloat16)
        return 0

    lax.fori_loop(0, 2, product, 0)
    w_copy.wait()
    to_time = lax.broadcasted_iota(jnp.int32, (128, NEV), 0) >> 3
    sent_ref[...] = jnp.zeros((128, NEV), jnp.float32)

    def trace(slot, _):
        acc_ref[...] = jnp.zeros_like(acc_ref)

        for h in range(CHUNKS):
            q_copy(slot, h).wait()
            lhs = jnp.concatenate([p_ref[slot, h * size + n] for n in range(size)], axis=1)
            rhs = jnp.concatenate([q_ref[slot, h * size + n] for n in range(size)], axis=1)
            acc_ref[...] += dot_nt(lhs, rhs)
        sums = []
        for w in range(2):
            total = 0.0
            for r in range(16):
                rows = slice(16 * r, 16 * r + 16)
                total = total + acc_ref[rows, :] * w_ref[w, rows, :].astype(jnp.float32)
            sums.append(total[:8] + total[8:])
        parts = []
        for part in range(3):
            parts.append([total.astype(jnp.bfloat16) for total in sums])
            sums = [total - low.astype(jnp.float32) for total, low in zip(sums, parts[-1])]
        stacked = jnp.concatenate(
            [jnp.concatenate(pair, axis=1).astype(jnp.float32) for pair in parts], axis=0
        ).astype(jnp.bfloat16)
        row = lax.broadcasted_iota(jnp.int32, (512, 2 * NEV), 0)
        lane = lax.broadcasted_iota(jnp.int32, (512, 2 * NEV), 1)
        j_lane = jnp.where(lane < NEV, lane >> 1 & 7, lane >> 4 & 7)
        kept = (j_lane == (row >> 5 & 7)) & ((lane & 1) == (row >> 8))
        spread = jnp.dot(
            stacked,
            jnp.where(kept, 1.0, 0.0).astype(jnp.bfloat16),
            preferred_element_type=jnp.float32,
        )
        spread = (spread[16:24] + spread[8:16]) + spread[0:8]
        lane8 = lax.broadcasted_iota(jnp.int32, (8, 2 * NEV), 1)
        row8 = lax.broadcasted_iota(jnp.int32, (8, 2 * NEV), 0)
        i_lane = jnp.where(lane8 < NEV, lane8 >> 4 & 7, lane8 >> 1 & 7)
        both = jnp.sum(jnp.where(i_lane == row8, spread, 0.0), axis=0, keepdims=True)
        own_ref[slot] = jnp.broadcast_to(both[:, :NEV], (8, NEV))
        here = to_time == times_ref[place_ref[1] * 2 + slot]
        sent_ref[...] = jnp.where(here, both[:, NEV:], sent_ref[...])
        return 0

    lax.fori_loop(0, 2, trace, 0)


def sink_side(scalars, elemental, tau_cols, weights, q_rows):
    smem = pl.BlockSpec(memory_space=pltpu.SMEM)
    vmem = pl.BlockSpec(memory_space=pltpu.VMEM)
    hbm = pl.BlockSpec(memory_space=pltpu.HBM)
    return pl.pallas_call(
        sink_kernel,
        out_shape=[
            jax.ShapeDtypeStruct((2, 8, NEV), jnp.float32),
            jax.ShapeDtypeStruct((128, NEV), jnp.float32),
        ],
        in_specs=[smem] * 4 + [vmem, hbm, hbm, hbm],
        out_specs=[vmem] * 2,
        scratch_shapes=[
            pltpu.VMEM((1024, 2 * NEV), jnp.bfloat16),
            pltpu.VMEM((2, 2, 16, NEV, NEV), jnp.bfloat16),
            pltpu.VMEM((2, NEV, 256, NEV), jnp.bfloat16),
            pltpu.VMEM((2, NEV, 256, NEV), jnp.bfloat16),
            pltpu.VMEM((256, 256), jnp.float32),
            pltpu.VMEM((2, 256, 256), jnp.bfloat16),
            pltpu.SemaphoreType.DMA((3,)),
            pltpu.SemaphoreType.DMA((2, CHUNKS)),
        ],
        compiler_params=pltpu.CompilerParams(vmem_limit_bytes=VMEM_LIMIT),
        cost_estimate=pl.CostEstimate(
            flops=8 * 2048 * 256 * 2048, bytes_accessed=20 * 1024 * 1024, transcendentals=0
        ),
        name="sink_side",
    )(*scalars, elemental, tau_cols, weights, q_rows)


def average_kernel(times_ref, place_ref, arrived_ref, own_ref, out_ref):
    slots = own_ref.shape[0]
    here = jnp.int32(0)
    for slot in range(times_ref.shape[0]):
        here = here + jnp.where(times_ref[slot] == place_ref[0], slot, 0)
    lane = lax.broadcasted_iota(jnp.int32, (16, NEV), 1)
    row = lax.broadcasted_iota(jnp.int32, (16, NEV), 0)
    kept = ((lane >> 4) == (row >> 1)) & ((lane & 1) == (row & 1))
    from_lane = lax.broadcasted_iota(jnp.int32, (NEV, NEV), 0) >> 1 & 7
    to_lane = lax.broadcasted_iota(jnp.int32, (NEV, NEV), 1)
    fold = (from_lane == to_lane).astype(jnp.float32)
    for slot in range(slots):
        at = times_ref[place_ref[1] * slots + slot] * 8 + here // slots
        mean = 0.5 * (own_ref[slot, 0:1, :] + arrived_ref[at])
        spread = jnp.where(kept, jnp.broadcast_to(mean, (16, NEV)), 0.0)
        folded = jnp.dot(spread, fold, precision=HIGH, preferred_element_type=jnp.float32)
        for i in range(OPS):
            out_ref[slot, i] = folded[2 * i : 2 * i + 2, :OPS]


def average(sink_times, place, arrived, own):
    smem = pl.BlockSpec(memory_space=pltpu.SMEM)
    vmem = pl.BlockSpec(memory_space=pltpu.VMEM)
    return pl.pallas_call(
        average_kernel,
        out_shape=jax.ShapeDtypeStruct((own.shape[0], OPS, 2, OPS), jnp.float32),
        in_specs=[smem, smem, vmem, vmem],
        out_specs=vmem,
        name="average",
    )(sink_times, place, arrived, own)


def shards(perambulators, elementals, gamma_codes, momenta, displacements, sink_times):
    slots = perambulators.shape[1]
    src_index = lax.axis_index("src")
    snk_index = lax.axis_index("snk")
    place = jnp.stack([src_index, snk_index]).astype(jnp.int32)
    source_elem = elementals[0]

    spread = lax.all_to_all(source_elem.reshape(16, NEV, NEV), "src", 0, 0, tiled=True)
    tau_rows = perambulators[0].transpose(0, 1, 3, 2, 4, 5).reshape(slots, 2, 2048, NEV)
    tau_cols = perambulators[0].transpose(0, 1, 2, 4, 3, 5).reshape(slots, 2, 16, NEV, NEV)
    weights = mixing_weights(gamma_codes)
    spread = spread.reshape(16, NEV, NEV)
    sent = slot_parts(sink_times, place, spread, (tau_rows, tau_cols, weights))
    sink_elems = lax.all_to_all(sent, "src", 0, 0, tiled=True)
    q_rows = source_side(momenta, displacements, tau_rows, source_elem)
    scalars = (sink_times, place, momenta, displacements)
    own, mirror = sink_side(scalars, sink_elems, tau_cols, weights, q_rows)
    arrived = lax.all_to_all(mirror[:, None], BOTH, 0, 0, tiled=True)
    result = average(sink_times, place, arrived, own)
    return result.transpose(0, 1, 3, 2)[None]


def solution(mesh):
    in_specs = (
        P("src", "snk", None, None, None, None, None),
        P("src", None, None, None, None),
        P(),
        P(),
        P(),
        P(),
    )
    out_specs = P("src", "snk", None, None, None)
    return jax.shard_map(shards, mesh=mesh, in_specs=in_specs, out_specs=out_specs, check_vma=False)
```

```python
import jax
import jax.numpy as jnp
import numpy as np
from jax import lax
from jax.experimental import pallas as pl
from jax.experimental.pallas import tpu as pltpu
from jax.sharding import PartitionSpec as P

NDISP = 2
NEV = 128
OPS = 8
BOTH = ("src", "snk")
HIGH = lax.Precision.HIGHEST
VMEM_LIMIT = 56 * 1024 * 1024
FULL_VMEM = 127 * 512 * 1024


def off_diagonal(upper, lower):
    return np.array(
        [
            [0, 0, upper[0, 0], upper[0, 1]],
            [0, 0, upper[1, 0], upper[1, 1]],
            [lower[0, 0], lower[0, 1], 0, 0],
            [lower[1, 0], lower[1, 1], 0, 0],
        ],
        dtype=complex,
    )


def gamma_tables():
    paulis = [
        np.array([[0, 1], [1, 0]], dtype=complex),
        np.array([[0, -1j], [1j, 0]], dtype=complex),
        np.array([[1, 0], [0, -1]], dtype=complex),
    ]
    identity = np.eye(2, dtype=complex)
    gammas = [off_diagonal(-1j * matrix, 1j * matrix) for matrix in paulis]
    gammas.append(off_diagonal(identity, identity))
    gamma_table = []
    for gamma_code in range(16):
        product = np.eye(4, dtype=complex)
        for bit_index in range(4):
            if gamma_code >> bit_index & 1:
                product = product @ gammas[bit_index]
        gamma_table.append(product)
    return np.stack(gamma_table)


def phase_table():
    table = gamma_tables()
    numbers = []
    for code in range(16):
        rows = [int(np.argmax(np.abs(table[code][:, col]))) for col in range(4)]
        phases = [
            int(np.round(np.angle(table[code][rows[col], col]) / (np.pi / 2))) % 4
            for col in range(4)
        ]
        numbers += phases + [rows[0]]
    return np.array(numbers, np.int32)


def weights_kernel(code_ref, table_ref, w_ref):
    row = lax.broadcasted_iota(jnp.int32, (256, NEV), 0)
    row_a, row_b, row_i = row >> 5 & 3, row >> 3 & 3, row & 7
    row_phase, row_xor = row >> 7, jnp.zeros_like(row)
    col = lax.broadcasted_iota(jnp.int32, (8, 256), 1)
    col_j, col_a, col_b = col >> 5, col >> 2 & 3, col & 3
    col_phase = (col >> 4 & 1) + 2 * ((col_a >> 1) ^ (col_b >> 1))
    col_xor = jnp.zeros_like(col)
    for op in range(OPS):
        base = code_ref[op] * 5
        row_xor = jnp.where(row_i == op, table_ref[base + 4], row_xor)
        col_xor = jnp.where(col_j == op, table_ref[base + 4], col_xor)
        for spin in range(4):
            phase = table_ref[base + spin]
            row_phase += jnp.where((row_i == op) & (row_a == spin), phase, 0)
            col_phase += jnp.where((col_j == op) & (col_b == spin), phase, 0)
    for half in range(2):
        lanes = slice(half * NEV, (half + 1) * NEV)
        shape = (256, NEV)
        c_phase = jnp.broadcast_to(col_phase[:1, lanes], shape)
        c_xor = jnp.broadcast_to(col_xor[:1, lanes], shape)
        c_a = jnp.broadcast_to(col_a[:1, lanes], shape)
        c_b = jnp.broadcast_to(col_b[:1, lanes], shape)
        kept = ((row_a ^ c_a) == row_xor) & ((row_b ^ c_b) == c_xor)
        phase = (row_phase + c_phase) & 3
        size = jnp.where(kept, 1.0, 0.0)
        sign = jnp.where(phase >= 2, -size, size)
        odd = (phase & 1) == 1
        w_ref[0, :, lanes] = jnp.where(odd, 0.0, sign).astype(jnp.bfloat16)
        w_ref[1, :, lanes] = jnp.where(odd, sign, 0.0).astype(jnp.bfloat16)


def mixing_weights(gamma_codes):
    smem = pl.BlockSpec(memory_space=pltpu.SMEM)
    vmem = pl.BlockSpec(memory_space=pltpu.VMEM)
    return pl.pallas_call(
        weights_kernel,
        out_shape=jax.ShapeDtypeStruct((2, 256, 256), jnp.bfloat16),
        in_specs=[smem, smem],
        out_specs=vmem,
        compiler_params=pltpu.CompilerParams(vmem_limit_bytes=FULL_VMEM),
        name="mixing_weights",
    )(gamma_codes, jnp.asarray(phase_table()))


def dot_nt(left, right):
    return lax.dot_general(
        left, right, (((1,), (1,)), ((), ())), preferred_element_type=jnp.float32
    )


def slot_parts_kernel(times_ref, place_ref, spread_ref, *refs):
    out_ref, held_ref, sem = refs[-3:]
    for slot in range(2):
        held_ref[slot] = spread_ref[times_ref[place_ref[1] * 2 + slot]]
    copies = [pltpu.make_async_copy(held_ref, out_ref.at[s], sem.at[s]) for s in range(16)]
    for copy in copies:
        copy.start()
    for copy in copies:
        copy.wait()


def slot_parts(sink_times, place, spread, before):
    smem = pl.BlockSpec(memory_space=pltpu.SMEM)
    hbm = pl.BlockSpec(memory_space=pltpu.HBM)
    return pl.pallas_call(
        slot_parts_kernel,
        out_shape=jax.ShapeDtypeStruct((16, 2, NEV, NEV), jnp.bfloat16),
        in_specs=[smem, smem, pl.BlockSpec(memory_space=pltpu.VMEM)] + [hbm] * len(before),
        out_specs=hbm,
        scratch_shapes=[
            pltpu.VMEM((2, NEV, NEV), jnp.bfloat16),
            pltpu.SemaphoreType.DMA((16,)),
        ],
        name="slot_parts",
    )(sink_times, place, spread, *before)


def source_kernel(momenta_ref, displacements_ref, tau_ref, el_ref, *refs):
    out_ref, held_ref, sems = refs

    def copy_of(slot, part):
        rows = slice(64 * part, 64 * (part + 1))
        return pltpu.make_async_copy(
            held_ref.at[slot, :, rows], out_ref.at[slot, :, rows], sems.at[slot, part]
        )

    def product(slot, _):
        lhs = jnp.concatenate([tau_ref[slot, 0], tau_ref[slot, 1]], axis=1)
        for j in range(OPS):
            e = momenta_ref[j] * NDISP + displacements_ref[j]
            b_real, b_imag = el_ref[e, 0], el_ref[e, 1]
            weight = jnp.concatenate(
                [
                    jnp.concatenate([b_real, b_imag], axis=1),
                    jnp.concatenate([b_imag, -b_real], axis=1),
                ],
                axis=0,
            )
            result = dot_nt(lhs, weight)
            for c in range(2):
                row = (2 * j + c) * 16
                part = result[:, c * NEV : (c + 1) * NEV].reshape(NEV, 16, NEV)
                held_ref[slot, :, row : row + 16, :] = part.astype(jnp.bfloat16)
            if j % 2 == 1:
                copy_of(slot, j // 2).start()
        return 0

    lax.fori_loop(0, 2, product, 0)
    for slot in range(2):
        for part in range(4):
            copy_of(slot, part).wait()


def source_side(momenta, displacements, tau_rows, elemental):
    smem = pl.BlockSpec(memory_space=pltpu.SMEM)
    vmem = pl.BlockSpec(memory_space=pltpu.VMEM)
    hbm = pl.BlockSpec(memory_space=pltpu.HBM)
    return pl.pallas_call(
        source_kernel,
        out_shape=jax.ShapeDtypeStruct((2, NEV, 256, NEV), jnp.bfloat16),
        in_specs=[smem, smem, vmem, vmem],
        out_specs=hbm,
        scratch_shapes=[
            pltpu.VMEM((2, NEV, 256, NEV), jnp.bfloat16),
            pltpu.SemaphoreType.DMA((2, 4)),
        ],
        compiler_params=pltpu.CompilerParams(vmem_limit_bytes=FULL_VMEM),
        cost_estimate=pl.CostEstimate(
            flops=4 * 2048 * 256 * 2048, bytes_accessed=20 * 1024 * 1024, transcendentals=0
        ),
        name="source_side",
    )(momenta, displacements, tau_rows, elemental)


CHUNKS = 1


def sink_kernel(times_ref, place_ref, momenta_ref, displacements_ref, *refs):
    el_hbm, tau_hbm, w_hbm, q_hbm, own_ref, sent_ref, *refs = refs
    el_ref, left_ref, tau_ref, p_ref, q_ref, acc_ref, w_ref, load_sems, q_sems = refs
    size = NEV // CHUNKS

    def tau_copy(slot):
        return pltpu.make_async_copy(tau_hbm.at[slot], tau_ref.at[slot], load_sems.at[slot])

    w_copy = pltpu.make_async_copy(w_hbm, w_ref, load_sems.at[2])
    el_copy = pltpu.make_async_copy(el_hbm, el_ref, load_sems.at[3])
    el_copy.start()

    def q_copy(slot, h):
        part = pl.ds(h * size, size)
        return pltpu.make_async_copy(
            q_hbm.at[slot, part], q_ref.at[slot, part], q_sems.at[slot, h]
        )

    for slot in range(2):
        tau_copy(slot).start()
        for h in range(CHUNKS):
            q_copy(slot, h).start()
    w_copy.start()
    el_copy.wait()

    def product(slot, _):
        elems = [momenta_ref[i] * NDISP + displacements_ref[i] for i in range(OPS)]

        def arrange(block, _):
            at = pl.ds(pl.multiple_of(16 * block, 16), 16)
            parts = [
                jnp.concatenate([el_ref[2 * e + c, slot, at, :] for c in range(2)], axis=1)
                for e in elems
            ]
            rows = jnp.swapaxes(jnp.stack(parts).astype(jnp.float32), 0, 1)
            rows = rows.reshape(128, 2 * NEV).astype(jnp.bfloat16)
            left_ref[pl.ds(pl.multiple_of(128 * block, 128), 128), :] = rows
            return 0

        lax.fori_loop(0, 8, arrange, 0)
        tau_copy(slot).wait()
        for c in range(2):
            for g in range(8):
                tiles = []
                for ab in range(2):
                    t_real, t_imag = tau_ref[slot, 0, 2 * g + ab], tau_ref[slot, 1, 2 * g + ab]
                    upper, lower = (t_real, -t_imag) if c == 0 else (t_imag, t_real)
                    tiles.append(jnp.concatenate([upper, lower], axis=0))
                result = jnp.dot(
                    left_ref[...],
                    jnp.concatenate(tiles, axis=1),
                    preferred_element_type=jnp.float32,
                )
                both = jnp.concatenate(
                    [
                        result[:, :NEV].reshape(NEV, OPS, NEV),
                        result[:, NEV:].reshape(NEV, OPS, NEV),
                    ],
                    axis=1,
                )
                row = c * 128 + g * 16
                p_ref[slot, :, row : row + 16, :] = both.astype(jnp.bfloat16)
        return 0

    lax.fori_loop(0, 2, product, 0)
    w_copy.wait()
    to_time = lax.broadcasted_iota(jnp.int32, (128, NEV), 0) >> 3
    sent_ref[...] = jnp.zeros((128, NEV), jnp.float32)

    def trace(slot, _):
        acc_ref[...] = jnp.zeros_like(acc_ref)

        for h in range(CHUNKS):
            q_copy(slot, h).wait()
            lhs = jnp.concatenate([p_ref[slot, h * size + n] for n in range(size)], axis=1)
            rhs = jnp.concatenate([q_ref[slot, h * size + n] for n in range(size)], axis=1)
            acc_ref[...] += dot_nt(lhs, rhs)
        sums = []
        for w in range(2):
            total = 0.0
            for r in range(16):
                rows = slice(16 * r, 16 * r + 16)
                total = total + acc_ref[rows, :] * w_ref[w, rows, :].astype(jnp.float32)
            sums.append(total[:8] + total[8:])
        parts = []
        for part in range(3):
            parts.append([total.astype(jnp.bfloat16) for total in sums])
            sums = [total - low.astype(jnp.float32) for total, low in zip(sums, parts[-1])]
        stacked = jnp.concatenate(
            [jnp.concatenate(pair, axis=1).astype(jnp.float32) for pair in parts], axis=0
        ).astype(jnp.bfloat16)
        row = lax.broadcasted_iota(jnp.int32, (512, 2 * NEV), 0)
        lane = lax.broadcasted_iota(jnp.int32, (512, 2 * NEV), 1)
        j_lane = jnp.where(lane < NEV, lane >> 1 & 7, lane >> 4 & 7)
        kept = (j_lane == (row >> 5 & 7)) & ((lane & 1) == (row >> 8))
        spread = jnp.dot(
            stacked,
            jnp.where(kept, 1.0, 0.0).astype(jnp.bfloat16),
            preferred_element_type=jnp.float32,
        )
        spread = (spread[16:24] + spread[8:16]) + spread[0:8]
        lane8 = lax.broadcasted_iota(jnp.int32, (8, 2 * NEV), 1)
        row8 = lax.broadcasted_iota(jnp.int32, (8, 2 * NEV), 0)
        i_lane = jnp.where(lane8 < NEV, lane8 >> 4 & 7, lane8 >> 1 & 7)
        both = jnp.sum(jnp.where(i_lane == row8, spread, 0.0), axis=0, keepdims=True)
        own_ref[slot] = jnp.broadcast_to(both[:, :NEV], (8, NEV))
        here = to_time == times_ref[place_ref[1] * 2 + slot]
        sent_ref[...] = jnp.where(here, both[:, NEV:], sent_ref[...])
        return 0

    lax.fori_loop(0, 2, trace, 0)


def sink_side(scalars, elemental, tau_cols, weights, q_rows):
    smem = pl.BlockSpec(memory_space=pltpu.SMEM)
    vmem = pl.BlockSpec(memory_space=pltpu.VMEM)
    hbm = pl.BlockSpec(memory_space=pltpu.HBM)
    return pl.pallas_call(
        sink_kernel,
        out_shape=[
            jax.ShapeDtypeStruct((2, 8, NEV), jnp.float32),
            jax.ShapeDtypeStruct((128, NEV), jnp.float32),
        ],
        in_specs=[smem] * 4 + [hbm] * 4,
        out_specs=[vmem] * 2,
        scratch_shapes=[
            pltpu.VMEM((16, 2, NEV, NEV), jnp.bfloat16),
            pltpu.VMEM((1024, 2 * NEV), jnp.bfloat16),
            pltpu.VMEM((2, 2, 16, NEV, NEV), jnp.bfloat16),
            pltpu.VMEM((2, NEV, 256, NEV), jnp.bfloat16),
            pltpu.VMEM((2, NEV, 256, NEV), jnp.bfloat16),
            pltpu.VMEM((256, 256), jnp.float32),
            pltpu.VMEM((2, 256, 256), jnp.bfloat16),
            pltpu.SemaphoreType.DMA((4,)),
            pltpu.SemaphoreType.DMA((2, CHUNKS)),
        ],
        compiler_params=pltpu.CompilerParams(vmem_limit_bytes=VMEM_LIMIT),
        cost_estimate=pl.CostEstimate(
            flops=8 * 2048 * 256 * 2048, bytes_accessed=20 * 1024 * 1024, transcendentals=0
        ),
        name="sink_side",
    )(*scalars, elemental, tau_cols, weights, q_rows)


def average_kernel(times_ref, place_ref, arrived_ref, own_ref, out_ref):
    slots = own_ref.shape[0]
    here = jnp.int32(0)
    for slot in range(times_ref.shape[0]):
        here = here + jnp.where(times_ref[slot] == place_ref[0], slot, 0)
    lane = lax.broadcasted_iota(jnp.int32, (16, NEV), 1)
    row = lax.broadcasted_iota(jnp.int32, (16, NEV), 0)
    kept = ((lane >> 4) == (row >> 1)) & ((lane & 1) == (row & 1))
    from_lane = lax.broadcasted_iota(jnp.int32, (NEV, NEV), 0) >> 1 & 7
    to_lane = lax.broadcasted_iota(jnp.int32, (NEV, NEV), 1)
    fold = (from_lane == to_lane).astype(jnp.float32)
    for slot in range(slots):
        at = times_ref[place_ref[1] * slots + slot] * 8 + here // slots
        mean = 0.5 * (own_ref[slot, 0:1, :] + arrived_ref[at])
        spread = jnp.where(kept, jnp.broadcast_to(mean, (16, NEV)), 0.0)
        folded = jnp.dot(spread, fold, precision=HIGH, preferred_element_type=jnp.float32)
        for i in range(OPS):
            out_ref[slot, i] = folded[2 * i : 2 * i + 2, :OPS]


def average(sink_times, place, arrived, own):
    smem = pl.BlockSpec(memory_space=pltpu.SMEM)
    vmem = pl.BlockSpec(memory_space=pltpu.VMEM)
    return pl.pallas_call(
        average_kernel,
        out_shape=jax.ShapeDtypeStruct((own.shape[0], OPS, 2, OPS), jnp.float32),
        in_specs=[smem, smem, vmem, vmem],
        out_specs=vmem,
        name="average",
    )(sink_times, place, arrived, own)


def shards(perambulators, elementals, gamma_codes, momenta, displacements, sink_times):
    slots = perambulators.shape[1]
    src_index = lax.axis_index("src")
    snk_index = lax.axis_index("snk")
    place = jnp.stack([src_index, snk_index]).astype(jnp.int32)
    source_elem = elementals[0]

    spread = lax.all_to_all(source_elem.reshape(16, NEV, NEV), "src", 0, 0, tiled=True)
    tau_rows = perambulators[0].transpose(0, 1, 3, 2, 4, 5).reshape(slots, 2, 2048, NEV)
    tau_cols = perambulators[0].transpose(0, 1, 2, 4, 3, 5).reshape(slots, 2, 16, NEV, NEV)
    weights = mixing_weights(gamma_codes)
    spread = spread.reshape(16, NEV, NEV)
    sent = slot_parts(sink_times, place, spread, (tau_rows, tau_cols, weights))
    sink_elems = lax.all_to_all(sent, "src", 0, 0, tiled=True)
    q_rows = source_side(momenta, displacements, tau_rows, source_elem)
    scalars = (sink_times, place, momenta, displacements)
    own, mirror = sink_side(scalars, sink_elems, tau_cols, weights, q_rows)
    arrived = lax.all_to_all(mirror[:, None], BOTH, 0, 0, tiled=True)
    result = average(sink_times, place, arrived, own)
    return result.transpose(0, 1, 3, 2)[None]


def solution(mesh):
    in_specs = (
        P("src", "snk", None, None, None, None, None),
        P("src", None, None, None, None),
        P(),
        P(),
        P(),
        P(),
    )
    out_specs = P("src", "snk", None, None, None)
    return jax.shard_map(shards, mesh=mesh, in_specs=in_specs, out_specs=out_specs, check_vma=False)
```

```python
import jax
import jax.numpy as jnp
import numpy as np
from jax import lax
from jax.experimental import pallas as pl
from jax.experimental.pallas import tpu as pltpu
from jax.sharding import PartitionSpec as P

NDISP = 2
NEV = 128
OPS = 8
BOTH = ("src", "snk")
HIGH = lax.Precision.HIGHEST
VMEM_LIMIT = 56 * 1024 * 1024
FULL_VMEM = 127 * 512 * 1024


def off_diagonal(upper, lower):
    return np.array(
        [
            [0, 0, upper[0, 0], upper[0, 1]],
            [0, 0, upper[1, 0], upper[1, 1]],
            [lower[0, 0], lower[0, 1], 0, 0],
            [lower[1, 0], lower[1, 1], 0, 0],
        ],
        dtype=complex,
    )


def gamma_tables():
    paulis = [
        np.array([[0, 1], [1, 0]], dtype=complex),
        np.array([[0, -1j], [1j, 0]], dtype=complex),
        np.array([[1, 0], [0, -1]], dtype=complex),
    ]
    identity = np.eye(2, dtype=complex)
    gammas = [off_diagonal(-1j * matrix, 1j * matrix) for matrix in paulis]
    gammas.append(off_diagonal(identity, identity))
    gamma_table = []
    for gamma_code in range(16):
        product = np.eye(4, dtype=complex)
        for bit_index in range(4):
            if gamma_code >> bit_index & 1:
                product = product @ gammas[bit_index]
        gamma_table.append(product)
    return np.stack(gamma_table)


def phase_table():
    table = gamma_tables()
    numbers = []
    for code in range(16):
        rows = [int(np.argmax(np.abs(table[code][:, col]))) for col in range(4)]
        phases = [
            int(np.round(np.angle(table[code][rows[col], col]) / (np.pi / 2))) % 4
            for col in range(4)
        ]
        numbers += phases + [rows[0]]
    return np.array(numbers, np.int32)


def weights_kernel(code_ref, table_ref, w_ref):
    row = lax.broadcasted_iota(jnp.int32, (256, NEV), 0)
    row_a, row_b, row_i = row >> 5 & 3, row >> 3 & 3, row & 7
    row_phase, row_xor = row >> 7, jnp.zeros_like(row)
    col = lax.broadcasted_iota(jnp.int32, (8, 256), 1)
    col_j, col_a, col_b = col >> 5, col >> 2 & 3, col & 3
    col_phase = (col >> 4 & 1) + 2 * ((col_a >> 1) ^ (col_b >> 1))
    col_xor = jnp.zeros_like(col)
    for op in range(OPS):
        base = code_ref[op] * 5
        row_xor = jnp.where(row_i == op, table_ref[base + 4], row_xor)
        col_xor = jnp.where(col_j == op, table_ref[base + 4], col_xor)
        for spin in range(4):
            phase = table_ref[base + spin]
            row_phase += jnp.where((row_i == op) & (row_a == spin), phase, 0)
            col_phase += jnp.where((col_j == op) & (col_b == spin), phase, 0)
    for half in range(2):
        lanes = slice(half * NEV, (half + 1) * NEV)
        shape = (256, NEV)
        c_phase = jnp.broadcast_to(col_phase[:1, lanes], shape)
        c_xor = jnp.broadcast_to(col_xor[:1, lanes], shape)
        c_a = jnp.broadcast_to(col_a[:1, lanes], shape)
        c_b = jnp.broadcast_to(col_b[:1, lanes], shape)
        kept = ((row_a ^ c_a) == row_xor) & ((row_b ^ c_b) == c_xor)
        phase = (row_phase + c_phase) & 3
        size = jnp.where(kept, 1.0, 0.0)
        sign = jnp.where(phase >= 2, -size, size)
        odd = (phase & 1) == 1
        w_ref[0, :, lanes] = jnp.where(odd, 0.0, sign).astype(jnp.bfloat16)
        w_ref[1, :, lanes] = jnp.where(odd, sign, 0.0).astype(jnp.bfloat16)


def mixing_weights(gamma_codes):
    smem = pl.BlockSpec(memory_space=pltpu.SMEM)
    vmem = pl.BlockSpec(memory_space=pltpu.VMEM)
    return pl.pallas_call(
        weights_kernel,
        out_shape=jax.ShapeDtypeStruct((2, 256, 256), jnp.bfloat16),
        in_specs=[smem, smem],
        out_specs=vmem,
        compiler_params=pltpu.CompilerParams(vmem_limit_bytes=FULL_VMEM),
        name="mixing_weights",
    )(gamma_codes, jnp.asarray(phase_table()))


def dot_nt(left, right):
    return lax.dot_general(
        left, right, (((1,), (1,)), ((), ())), preferred_element_type=jnp.float32
    )


def slot_parts_kernel(times_ref, place_ref, spread_ref, *refs):
    out_ref, held_ref, sem = refs[-3:]
    for slot in range(2):
        held_ref[slot] = spread_ref[times_ref[place_ref[1] * 2 + slot]]
    copies = [pltpu.make_async_copy(held_ref, out_ref.at[s], sem.at[s]) for s in range(16)]
    for copy in copies:
        copy.start()
    for copy in copies:
        copy.wait()


def slot_parts(sink_times, place, spread, before):
    smem = pl.BlockSpec(memory_space=pltpu.SMEM)
    hbm = pl.BlockSpec(memory_space=pltpu.HBM)
    return pl.pallas_call(
        slot_parts_kernel,
        out_shape=jax.ShapeDtypeStruct((16, 2, NEV, NEV), jnp.bfloat16),
        in_specs=[smem, smem, pl.BlockSpec(memory_space=pltpu.VMEM)] + [hbm] * len(before),
        out_specs=hbm,
        scratch_shapes=[
            pltpu.VMEM((2, NEV, NEV), jnp.bfloat16),
            pltpu.SemaphoreType.DMA((16,)),
        ],
        name="slot_parts",
    )(sink_times, place, spread, *before)


def source_kernel(momenta_ref, displacements_ref, tau_ref, el_ref, *refs):
    out_ref, held_ref, sems = refs

    def copy_of(slot, part):
        rows = slice(64 * part, 64 * (part + 1))
        return pltpu.make_async_copy(
            held_ref.at[slot, :, rows], out_ref.at[slot, :, rows], sems.at[slot, part]
        )

    def product(slot, _):
        lhs = jnp.concatenate([tau_ref[slot, 0], tau_ref[slot, 1]], axis=1)
        for j in range(OPS):
            e = momenta_ref[j] * NDISP + displacements_ref[j]
            b_real, b_imag = el_ref[e, 0], el_ref[e, 1]
            weight = jnp.concatenate(
                [
                    jnp.concatenate([b_real, b_imag], axis=1),
                    jnp.concatenate([b_imag, -b_real], axis=1),
                ],
                axis=0,
            )
            result = dot_nt(lhs, weight)
            for c in range(2):
                row = (2 * j + c) * 16
                part = result[:, c * NEV : (c + 1) * NEV].reshape(NEV, 16, NEV)
                held_ref[slot, :, row : row + 16, :] = part.astype(jnp.bfloat16)
            if j % 2 == 1:
                copy_of(slot, j // 2).start()
        return 0

    lax.fori_loop(0, 2, product, 0)
    for slot in range(2):
        for part in range(4):
            copy_of(slot, part).wait()


def source_side(momenta, displacements, tau_rows, elemental):
    smem = pl.BlockSpec(memory_space=pltpu.SMEM)
    vmem = pl.BlockSpec(memory_space=pltpu.VMEM)
    hbm = pl.BlockSpec(memory_space=pltpu.HBM)
    return pl.pallas_call(
        source_kernel,
        out_shape=jax.ShapeDtypeStruct((2, NEV, 256, NEV), jnp.bfloat16),
        in_specs=[smem, smem, vmem, vmem],
        out_specs=hbm,
        scratch_shapes=[
            pltpu.VMEM((2, NEV, 256, NEV), jnp.bfloat16),
            pltpu.SemaphoreType.DMA((2, 4)),
        ],
        compiler_params=pltpu.CompilerParams(vmem_limit_bytes=FULL_VMEM),
        cost_estimate=pl.CostEstimate(
            flops=4 * 2048 * 256 * 2048, bytes_accessed=20 * 1024 * 1024, transcendentals=0
        ),
        name="source_side",
    )(momenta, displacements, tau_rows, elemental)


CHUNKS = 1


def sink_kernel(times_ref, place_ref, momenta_ref, displacements_ref, *refs):
    el_hbm, tau_hbm, w_hbm, q_hbm, own_ref, sent_ref, *refs = refs
    el_ref, left_ref, tau_ref, p_ref, q_ref, acc_ref, w_ref, load_sems, q_sems = refs
    size = NEV // CHUNKS

    def tau_copy(slot):
        return pltpu.make_async_copy(tau_hbm.at[slot], tau_ref.at[slot], load_sems.at[slot])

    w_copy = pltpu.make_async_copy(w_hbm, w_ref, load_sems.at[2])
    el_copy = pltpu.make_async_copy(el_hbm, el_ref, load_sems.at[3])
    el_copy.start()

    def q_copy(slot, h):
        part = pl.ds(h * size, size)
        return pltpu.make_async_copy(
            q_hbm.at[slot, part], q_ref.at[slot, part], q_sems.at[slot, h]
        )

    for slot in range(2):
        tau_copy(slot).start()
        for h in range(CHUNKS):
            q_copy(slot, h).start()
    w_copy.start()
    el_copy.wait()

    def product(slot, _):
        elems = [momenta_ref[i] * NDISP + displacements_ref[i] for i in range(OPS)]

        def arrange(block, _):
            at = pl.ds(pl.multiple_of(16 * block, 16), 16)
            parts = [
                jnp.concatenate([el_ref[2 * e + c, slot, at, :] for c in range(2)], axis=1)
                for e in elems
            ]
            rows = jnp.swapaxes(jnp.stack(parts).astype(jnp.float32), 0, 1)
            rows = rows.reshape(128, 2 * NEV).astype(jnp.bfloat16)
            left_ref[pl.ds(pl.multiple_of(128 * block, 128), 128), :] = rows
            return 0

        lax.fori_loop(0, 8, arrange, 0)
        tau_copy(slot).wait()
        for c in range(2):
            for g in range(8):
                tiles = []
                for ab in range(2):
                    t_real, t_imag = tau_ref[slot, 0, 2 * g + ab], tau_ref[slot, 1, 2 * g + ab]
                    upper, lower = (t_real, -t_imag) if c == 0 else (t_imag, t_real)
                    tiles.append(jnp.concatenate([upper, lower], axis=0))
                result = jnp.dot(
                    left_ref[...],
                    jnp.concatenate(tiles, axis=1),
                    preferred_element_type=jnp.float32,
                )
                both = jnp.concatenate(
                    [
                        result[:, :NEV].reshape(NEV, OPS, NEV),
                        result[:, NEV:].reshape(NEV, OPS, NEV),
                    ],
                    axis=1,
                )
                row = c * 128 + g * 16
                p_ref[slot, :, row : row + 16, :] = both.astype(jnp.bfloat16)
        return 0

    lax.fori_loop(0, 2, product, 0)
    w_copy.wait()
    to_time = lax.broadcasted_iota(jnp.int32, (128, NEV), 0) >> 3
    sent_ref[...] = jnp.zeros((128, NEV), jnp.float32)

    def trace(slot, _):
        acc_ref[...] = jnp.zeros_like(acc_ref)

        for h in range(CHUNKS):
            q_copy(slot, h).wait()
            lhs = jnp.concatenate([p_ref[slot, h * size + n] for n in range(size)], axis=1)
            rhs = jnp.concatenate([q_ref[slot, h * size + n] for n in range(size)], axis=1)
            acc_ref[...] += dot_nt(lhs, rhs)
        sums = []
        for w in range(2):
            total = 0.0
            for r in range(16):
                rows = slice(16 * r, 16 * r + 16)
                total = total + acc_ref[rows, :] * w_ref[w, rows, :].astype(jnp.float32)
            sums.append(total[:8] + total[8:])
        parts = []
        for part in range(3):
            parts.append([total.astype(jnp.bfloat16) for total in sums])
            sums = [total - low.astype(jnp.float32) for total, low in zip(sums, parts[-1])]
        stacked = jnp.concatenate(
            [jnp.concatenate(pair, axis=1).astype(jnp.float32) for pair in parts], axis=0
        ).astype(jnp.bfloat16)
        row = lax.broadcasted_iota(jnp.int32, (512, 2 * NEV), 0)
        lane = lax.broadcasted_iota(jnp.int32, (512, 2 * NEV), 1)
        j_lane = jnp.where(lane < NEV, lane & 7, lane >> 4 & 7)
        kept = (j_lane == (row >> 5 & 7)) & ((lane >> 3 & 1) == (row >> 8))
        spread = jnp.dot(
            stacked,
            jnp.where(kept, 1.0, 0.0).astype(jnp.bfloat16),
            preferred_element_type=jnp.float32,
        )
        spread = (spread[16:24] + spread[8:16]) + spread[0:8]
        lane8 = lax.broadcasted_iota(jnp.int32, (8, 2 * NEV), 1)
        row8 = lax.broadcasted_iota(jnp.int32, (8, 2 * NEV), 0)
        i_lane = jnp.where(lane8 < NEV, lane8 >> 4 & 7, lane8 & 7)
        both = jnp.sum(jnp.where(i_lane == row8, spread, 0.0), axis=0, keepdims=True)
        own_ref[slot] = jnp.broadcast_to(both[:, :NEV], (8, NEV))
        here = to_time == times_ref[place_ref[1] * 2 + slot]
        sent_ref[...] = jnp.where(here, both[:, NEV:], sent_ref[...])
        return 0

    lax.fori_loop(0, 2, trace, 0)


def sink_side(scalars, elemental, tau_cols, weights, q_rows):
    smem = pl.BlockSpec(memory_space=pltpu.SMEM)
    vmem = pl.BlockSpec(memory_space=pltpu.VMEM)
    hbm = pl.BlockSpec(memory_space=pltpu.HBM)
    return pl.pallas_call(
        sink_kernel,
        out_shape=[
            jax.ShapeDtypeStruct((2, 8, NEV), jnp.float32),
            jax.ShapeDtypeStruct((128, NEV), jnp.float32),
        ],
        in_specs=[smem] * 4 + [hbm] * 4,
        out_specs=[vmem] * 2,
        scratch_shapes=[
            pltpu.VMEM((16, 2, NEV, NEV), jnp.bfloat16),
            pltpu.VMEM((1024, 2 * NEV), jnp.bfloat16),
            pltpu.VMEM((2, 2, 16, NEV, NEV), jnp.bfloat16),
            pltpu.VMEM((2, NEV, 256, NEV), jnp.bfloat16),
            pltpu.VMEM((2, NEV, 256, NEV), jnp.bfloat16),
            pltpu.VMEM((256, 256), jnp.float32),
            pltpu.VMEM((2, 256, 256), jnp.bfloat16),
            pltpu.SemaphoreType.DMA((4,)),
            pltpu.SemaphoreType.DMA((2, CHUNKS)),
        ],
        compiler_params=pltpu.CompilerParams(vmem_limit_bytes=VMEM_LIMIT),
        cost_estimate=pl.CostEstimate(
            flops=8 * 2048 * 256 * 2048, bytes_accessed=20 * 1024 * 1024, transcendentals=0
        ),
        name="sink_side",
    )(*scalars, elemental, tau_cols, weights, q_rows)


def shards(perambulators, elementals, gamma_codes, momenta, displacements, sink_times):
    slots = perambulators.shape[1]
    src_index = lax.axis_index("src")
    snk_index = lax.axis_index("snk")
    place = jnp.stack([src_index, snk_index]).astype(jnp.int32)
    source_elem = elementals[0]

    spread = lax.all_to_all(source_elem.reshape(16, NEV, NEV), "src", 0, 0, tiled=True)
    tau_rows = perambulators[0].transpose(0, 1, 3, 2, 4, 5).reshape(slots, 2, 2048, NEV)
    tau_cols = perambulators[0].transpose(0, 1, 2, 4, 3, 5).reshape(slots, 2, 16, NEV, NEV)
    weights = mixing_weights(gamma_codes)
    spread = spread.reshape(16, NEV, NEV)
    sent = slot_parts(sink_times, place, spread, (tau_rows, tau_cols, weights))
    sink_elems = lax.all_to_all(sent, "src", 0, 0, tiled=True)
    q_rows = source_side(momenta, displacements, tau_rows, source_elem)
    scalars = (sink_times, place, momenta, displacements)
    own, mirror = sink_side(scalars, sink_elems, tau_cols, weights, q_rows)
    arrived = lax.all_to_all(mirror[:, None], BOTH, 0, 0, tiled=True)
    positions = jnp.arange(sink_times.shape[0], dtype=jnp.int32)
    here = jnp.sum(jnp.where(sink_times == src_index, positions, 0))
    times = lax.dynamic_slice_in_dim(sink_times, snk_index * slots, slots)
    places = times * 8 + (here >> 1)
    rows = [
        lax.dynamic_slice_in_dim(arrived[:, 0], places[slot], 1) for slot in range(slots)
    ]
    result = 0.5 * (own[:, 0] + jnp.concatenate(rows))
    return result.reshape(slots, OPS, 2, OPS).transpose(0, 1, 3, 2)[None]


def solution(mesh):
    in_specs = (
        P("src", "snk", None, None, None, None, None),
        P("src", None, None, None, None),
        P(),
        P(),
        P(),
        P(),
    )
    out_specs = P("src", "snk", None, None, None)
    return jax.shard_map(shards, mesh=mesh, in_specs=in_specs, out_specs=out_specs, check_vma=False)
```
